32 devices in a mesh: slide: 2 (over x), grid: 16 (over z, y, core).
Axes of the slice: x: 2, y: 2, z: 4, core: 2. Of those that a mesh axis runs over, the one named last changes fastest.
Arguments:
- embeddings: bfloat16 [2, 2048, 512], P('slide', 'grid'), may hold values from -6 to 6
- visible: int32 [2, 512], P('slide'), may hold values from 0 to 2047, as said below
- window_id: int32 [2, 2048], P('slide'), may hold values from 0 to 30, as said below
- output_gradient: bfloat16 [2, 2048, 512], P('slide', 'grid'), may hold values from -6 to 6
- mask_token: float32 [512], replicated, may hold values from -4 to 4
- enc_qkv: bfloat16 [512, 1536], replicated, may hold values from -2 to 2
- enc_out: bfloat16 [512, 512], replicated, may hold values from -0.25 to 0.25
- dec_qkv: bfloat16 [512, 1536], replicated, may hold values from -2 to 2
- decoder_projected: bfloat16 [512, 512], replicated, may hold values from -0.25 to 0.25
Outputs:
- grad_embeddings: bfloat16 [2, 2048, 512], P('slide', 'grid')
- grad_enc_out: float32 [512, 512], P('grid', 'slide')
- grad_dec_out: float32 [512, 512], P('grid', 'slide')
The draws below stay inside these ranges and needn't reach their ends.
Inputs may be any that keep to these rules, and one draw needn't show every extreme that they name: Each row holds 512 different tile numbers in ascending order. Visible tiles come in aligned runs of 32; in every slide all 128 tiles of one block of 128 aligned tiles are visible, and so are the runs that hold tiles 128 - 128 // 2 to 191. `window_id`: window numbers start at 0 in every slide and rise by 0 or 1 from tile to tile; a window holds 1 to 128 consecutive tiles; the last tile of every slide is in window 2 * 16 - 2.
All inputs are finite; a program needn't handle non-finite values.
Results may differ from the reference program's by a relative error of at most 0.019.
Values may be sent and summed in bfloat16 or wider, within the bound.
A program may use at most 64 MiB of HBM per device.

```python
import math
import jax
import jax.numpy as jnp
from jax import lax

D = 512
HEADS = 8
TILE_DEV = 128
WIN = 128
SLIDES = 2
TILES = 2048
VIS = 512
N_GRID = 16


def draw_visible(key, part):
    key = jax.random.fold_in(key, 11)
    run_len = TILE_DEV // 4
    runs_all = TILES // run_len
    chosen_count = VIS // run_len
    half = WIN // 2

    def one_slide(slide_key):
        first, second = jax.random.split(slide_key)
        full_shard = jax.random.randint(first, (), 0, TILES // TILE_DEV)
        logit_scores = jax.random.permutation(second, runs_all)
        run_ids = jnp.arange(runs_all)
        edge_run = (run_ids * run_len < TILE_DEV + half) & ((run_ids + 1) * run_len > TILE_DEV - half)
        forced = (run_ids // 4 == full_shard) | edge_run
        logit_scores = jnp.where(forced, runs_all + run_ids, logit_scores)
        picked = jnp.sort(lax.top_k(logit_scores, chosen_count)[1])
        tile_list = (picked[:, None] * run_len + jnp.arange(run_len)[None, :]).reshape(-1)
        return tile_list.astype(jnp.int32)
    return jax.vmap(one_slide)(jax.random.split(key, SLIDES))


def draw_window_id(key, part):
    key = jax.random.fold_in(key, 13)
    half = WIN // 2
    frame_count = TILES // WIN
    spots = jnp.arange(TILES, dtype=jnp.int32)
    shifted = spots - half
    frame_of = jnp.where(spots >= half, shifted // WIN, 0)
    offset_in = jnp.where(spots >= half, shifted % WIN, 0)
    frame_start = (spots == 0) | (spots >= half) & (offset_in == 0)
    full_frame = (spots >= half) & (half + (frame_of + 1) * WIN <= TILES)
    protected_frame = frame_of == (TILE_DEV - half - half) // WIN
    split_at = jax.random.randint(key, (SLIDES, frame_count), 1, WIN)
    chosen = jnp.take(split_at, jnp.clip(frame_of, 0, frame_count - 1), axis=1)
    extra = (offset_in[None, :] == chosen) & (full_frame & jnp.logical_not(protected_frame))[None, :]
    starts = frame_start[None, :] | extra
    return (jnp.cumsum(starts.astype(jnp.int32), axis=1) - 1).astype(jnp.int32)


def drawn_weights(key):
    return jnp.clip(jax.random.normal(key, (D, 3 * D), jnp.float32), -4.0, 4.0) * D ** (-0.5)


def draw_enc_qkv(key, part):
    key = jax.random.fold_in(key, 5)
    return drawn_weights(key).astype(jnp.bfloat16)


def draw_dec_qkv(key, part):
    key = jax.random.fold_in(key, 7)
    return drawn_weights(key).astype(jnp.bfloat16)


def block_levels(rng, dims, shards, smallest, high):
    loudness, own = 1.0, jax.random.fold_in(rng, 6)
    for dim, parts in shards:
        heights = jnp.exp(jax.random.uniform(jax.random.fold_in(own, dim), (parts,), jnp.float32, smallest / len(shards), high / len(shards)))
        loudness = loudness * jnp.repeat(heights, dims[dim] // parts).reshape([-1 if axis == dim else 1 for axis in range(len(dims))])
    return loudness


def scatter_about(rng, dims, spread, reach, cuts=(), held_as=jnp.bfloat16):
    gain = block_levels(rng, dims, cuts, -0.22, 0.18) if cuts else 1.0
    array = jax.random.normal(rng, dims, jnp.float32) * spread * gain
    return jnp.minimum(jnp.maximum(array, -reach), reach).astype(held_as)


def setup_inputs(seed: int = 0) -> dict:
    keys = jax.random.split(jax.random.key(seed), 10)
    return {
        "embeddings": scatter_about(keys[0], (SLIDES, TILES, D), 1.0, 6.0, ((0, 2), (1, 16))),
        "visible": draw_visible(jax.random.fold_in(keys[9], 71), 0),
        "window_id": draw_window_id(jax.random.fold_in(keys[9], 71), 0),
        "output_gradient": scatter_about(keys[3], (SLIDES, TILES, D), 1.0, 6.0, ((0, 2), (1, 16))),
        "mask_token": scatter_about(keys[4], (D,), 1.0, 4.0, (), jnp.float32),
        "enc_qkv": draw_enc_qkv(jax.random.fold_in(keys[9], 71), 0),
        "enc_out": scatter_about(keys[6], (D, D), D ** -0.5, 0.25),
        "dec_qkv": draw_dec_qkv(jax.random.fold_in(keys[9], 71), 0),
        "decoder_projected": scatter_about(keys[8], (D, D), D ** -0.5, 0.25),
    }


EPS = 1e-06

def rms_f(values):
    return values * lax.rsqrt(lax.optimization_barrier(jnp.mean(values * values, axis=-1, keepdims=True)) + EPS)

def attend(queries, key_vecs, values, allowed, head_count):
    shape_q = queries.shape
    head_width = shape_q[-1] // head_count
    query_per_head = queries.reshape(shape_q[:-1] + (head_count, head_width))
    key_per_head = key_vecs.reshape(key_vecs.shape[:-1] + (head_count, head_width))
    value_per_head = values.reshape(values.shape[:-1] + (head_count, head_width))
    logit_scores = jnp.einsum('...vys,...rys->...yvr', query_per_head, key_per_head) * (1.0 / math.sqrt(head_width))
    if allowed is not None:
        logit_scores = jnp.where(allowed[..., None, :, :], logit_scores, -1e+30)
    row_top = lax.stop_gradient(lax.optimization_barrier(jnp.max(logit_scores, axis=-1, keepdims=True)))
    weights = jnp.exp(logit_scores - row_top)
    attention_probs = (weights / lax.optimization_barrier(jnp.sum(weights, axis=-1, keepdims=True))).astype(jnp.bfloat16)
    attention_probs = lax.optimization_barrier(attention_probs).astype(jnp.float32)
    attended_rows = jnp.einsum('...wvy,...ywj->...vwj', attention_probs, value_per_head)
    return attended_rows.reshape(shape_q).astype(jnp.bfloat16)

def encoder_block(tokens, enc_qkv, enc_out):
    width = tokens.shape[-1]
    residual = tokens.astype(jnp.float32)
    normed = rms_f(residual).astype(jnp.bfloat16)
    projected = jnp.dot(normed, enc_qkv, preferred_element_type=jnp.float32).astype(jnp.bfloat16)
    projected = lax.optimization_barrier(projected).astype(jnp.float32)
    attended_rows = attend(projected[..., :width], projected[..., width:2 * width], projected[..., 2 * width:], None, HEADS)
    hidden = residual + jnp.dot(attended_rows, enc_out, preferred_element_type=jnp.float32)
    return (hidden.astype(jnp.bfloat16), attended_rows)

def decoder_grads(inputs, window, cotangent, dec_qkv, decoder_projected):
    length, width = inputs.shape
    block = math.gcd(length, 256)
    normed = rms_f(inputs).astype(jnp.bfloat16)
    queries = jnp.dot(normed, dec_qkv[:, :width], preferred_element_type=jnp.float32).astype(jnp.bfloat16)
    keyvals = jnp.dot(normed, dec_qkv[:, width:], preferred_element_type=jnp.float32).astype(jnp.bfloat16)
    queries, keyvals = lax.optimization_barrier((queries, keyvals))
    padded = jnp.pad(keyvals, ((WIN, WIN), (0, 0)))
    padded_ids = jnp.pad(window, (WIN, WIN), constant_values=-1)
    dcontext = jnp.dot(cotangent, decoder_projected.T, preferred_element_type=jnp.float32).astype(jnp.bfloat16)

    def step(carry, index):
        start = (index * block).astype(jnp.int32)
        query_block = lax.dynamic_slice_in_dim(queries, start, block, 0).astype(jnp.float32)
        keyval_block = lax.dynamic_slice_in_dim(padded, start, block + 2 * WIN, 0).astype(jnp.float32)
        query_ids = lax.dynamic_slice_in_dim(window, start, block, 0)
        key_ids = lax.dynamic_slice_in_dim(padded_ids, start, block + 2 * WIN, 0)
        allowed = query_ids[:, None] == key_ids[None, :]

        def window_attend(query_f, keyval_f):
            return attend(query_f, keyval_f[:, :width], keyval_f[:, width:], allowed, HEADS)
        attended_rows, back = jax.vjp(window_attend, query_block, keyval_block)
        grad_q, grad_kv = back(lax.dynamic_slice_in_dim(dcontext, start, block, 0))
        current = lax.dynamic_slice_in_dim(carry, start, block + 2 * WIN, 0)
        carry = lax.dynamic_update_slice_in_dim(carry, current + grad_kv, start, 0)
        return (carry, (grad_q, attended_rows))
    total_kv, (grad_q, attended_rows) = lax.scan(step, jnp.zeros((length + 2 * WIN, 2 * width), jnp.float32), jnp.arange(length // block, dtype=jnp.int32))
    grad_q = grad_q.reshape(length, width)
    attended_rows = attended_rows.reshape(length, width)
    grad_kv = total_kv[WIN:WIN + length]
    dnormed = jnp.dot(grad_q, dec_qkv[:, :width].T, precision=lax.Precision.HIGHEST, preferred_element_type=jnp.float32)
    dnormed = dnormed + jnp.dot(grad_kv, dec_qkv[:, width:].T, precision=lax.Precision.HIGHEST, preferred_element_type=jnp.float32)
    _, norm_back = jax.vjp(rms_f, inputs)
    dinputs = norm_back(dnormed)[0] + cotangent.astype(jnp.float32)
    grad_weight = jnp.dot(attended_rows.T, cotangent, preferred_element_type=jnp.float32)
    return (dinputs, grad_weight)

def reference(embeddings, visible, window_id, output_gradient, mask_token, enc_qkv, enc_out, dec_qkv, decoder_projected):

    def one_slide(operands):
        tile_rows, vis_list, window, cotangent = operands
        tokens = tile_rows[vis_list]
        grouped = tokens.reshape(VIS // N_GRID, N_GRID, D).transpose(1, 0, 2)

        def encode(inputs):
            return encoder_block(inputs, enc_qkv, enc_out)
        encoded, enc_back, encoder_attended = jax.vjp(encode, grouped, has_aux=True)
        encoded = lax.optimization_barrier(encoded)
        flat = encoded.transpose(1, 0, 2).reshape(VIS, D)
        inputs = jnp.broadcast_to(mask_token, (TILES, D)).astype(jnp.float32)
        inputs = inputs.at[vis_list].set(flat.astype(jnp.float32))
        dinputs, grad_dec = decoder_grads(inputs, window, cotangent, dec_qkv, decoder_projected)
        grad_flat = dinputs[vis_list].astype(jnp.bfloat16)
        grad_grouped = grad_flat.reshape(VIS // N_GRID, N_GRID, D).transpose(1, 0, 2)
        grad_enc = jnp.dot(encoder_attended.reshape(-1, D).T, grad_grouped.reshape(-1, D), preferred_element_type=jnp.float32)
        grad_tokens, = enc_back(grad_grouped)
        token_flat = grad_tokens.transpose(1, 0, 2).reshape(VIS, D)
        grad_tiles = jnp.zeros((TILES, D), jnp.bfloat16).at[vis_list].set(token_flat)
        return (grad_tiles, grad_enc, grad_dec)
    grad_tiles, enc_parts, dec_parts = lax.map(one_slide, (embeddings, visible, window_id, output_gradient))
    return (grad_tiles, lax.optimization_barrier(jnp.sum(enc_parts, axis=0)), lax.optimization_barrier(jnp.sum(dec_parts, axis=0)))
```

```python
import functools
import math

import jax
import jax.numpy as jnp
from jax import lax
from jax.experimental import pallas as pl
from jax.experimental.pallas import tpu as pltpu
from jax.sharding import PartitionSpec as P

HEADS = 8
EPS = 1e-06
CAP = 8
NEG = -1e30
BF = jnp.bfloat16
F32 = jnp.float32
I32 = jnp.int32
MESH = pl.DeviceIdType.MESH


def mm(a, b):
    return lax.dot_general(a, b, (((1,), (0,)), ((), ())), preferred_element_type=F32)


def mm_nt(a, b):
    return lax.dot_general(a, b, (((1,), (1,)), ((), ())), preferred_element_type=F32)


def mm_tn(a, b):
    return lax.dot_general(a, b, (((0,), (0,)), ((), ())), preferred_element_type=F32)


def iota(shape, dim):
    return lax.broadcasted_iota(I32, shape, dim)


def norm_scale(x):
    return lax.rsqrt(jnp.mean(x * x, axis=-1, keepdims=True) + EPS)


def norm_back(x, r, dn):
    return r * dn - x * (r * r * r * jnp.mean(dn * x, axis=-1, keepdims=True))


def pack(rows, peers):
    width = rows.shape[1]
    cube = rows.reshape(peers, CAP, width)
    halves = [cube[:, :, : width // 2], cube[:, :, width // 2 :]]
    return jnp.concatenate(halves, axis=1).astype(BF)


def unpack(cube):
    peers, rows, half = cube.shape
    wide = cube.astype(F32)
    wide = jnp.concatenate([wide[:, :CAP], wide[:, CAP:]], axis=2)
    return wide.reshape(peers * CAP, 2 * half).astype(BF)


def one_hot(ids, count):
    return jnp.where(iota((ids.shape[0], count), 1) == ids, 1.0, 0.0).astype(BF)


def as_columns(row):
    n = row.shape[1]
    return jnp.broadcast_to(row, (n, n)).T


def kernel(
    groups, slides, near,
    emb, vis, win, og, mask_token, enc_qkv, enc_out, dec_qkv, dec_out,
    out_tiles, out_enc, out_dec,
    sbuf, rbuf, og_halo, h_send, h_halo,
    dec_a_send, dec_b_send, dec_a, dec_b,
    enc_a_send, enc_b_send, enc_a, enc_b,
    far_send, far_recv, far_own, acc,
    a2a_ss, a2a_rs, halo_ss, halo_rs, near_ss, near_rs, far_ss, far_rs,
):
    s = lax.axis_index("slide")
    g = lax.axis_index("grid")
    tiles, width = emb.shape[1:]
    vis_all = vis.shape[1]
    tokens = vis_all // groups
    far = groups // near
    rb, cw = out_enc.shape
    n = lax.rem(g, near)
    f = lax.div(g, near)
    log_g = groups.bit_length() - 1
    pending = []

    barrier = pltpu.get_barrier_semaphore()
    met = 0
    for j in range(1, groups):
        pl.semaphore_signal(
            barrier, inc=1, device_id=(s, lax.rem(g + j, groups)), device_id_type=MESH
        )
        met += 1
    for ds in range(1, slides):
        for dn in range(near):
            peer = (lax.rem(s + ds, slides), f * near + lax.rem(n + dn, near))
            pl.semaphore_signal(barrier, inc=1, device_id=peer, device_id_type=MESH)
            met += 1

    def send(src, dst, ss, rs, peer):
        copy = pltpu.make_async_remote_copy(
            src_ref=src, dst_ref=dst, send_sem=ss, recv_sem=rs,
            device_id=peer, device_id_type=MESH,
        )
        copy.start()
        return copy

    def all_to_all_start(stage):
        copies = []
        for j in range(1, groups):
            dst = lax.rem(g + j, groups)
            copies.append(
                send(sbuf.at[stage, dst], rbuf.at[stage, g], a2a_ss.at[stage, j],
                     a2a_rs.at[stage, j], (s, dst))
            )
        rbuf[stage, g] = sbuf[stage, g]
        pending.extend(copies)
        return copies

    def all_to_all_wait(stage):
        for j in range(1, groups):
            src = lax.rem(g + groups - j, groups)
            pltpu.make_async_remote_copy(
                src_ref=sbuf.at[stage, src], dst_ref=rbuf.at[stage, src],
                send_sem=a2a_ss.at[stage, j], recv_sem=a2a_rs.at[stage, j],
                device_id=(s, src), device_id_type=MESH,
            ).wait_recv()
        return unpack(rbuf[stage])

    def halo_copies(kind, src, dst):
        left = jnp.maximum(g - 1, 0)
        right = jnp.minimum(g + 1, groups - 1)

        def to(side, peer):
            return pltpu.make_async_remote_copy(
                src_ref=src, dst_ref=dst.at[side], send_sem=halo_ss.at[kind, side],
                recv_sem=halo_rs.at[kind, side], device_id=(s, peer), device_id_type=MESH,
            )

        return to(1, left), to(0, right)

    def halo_start(kind, src, dst):
        to_left, to_right = halo_copies(kind, src, dst)

        @pl.when(g > 0)
        def _():
            to_left.start()

        @pl.when(g < groups - 1)
        def _():
            to_right.start()

    def halo_wait(kind, src, dst):
        to_left, to_right = halo_copies(kind, src, dst)

        @pl.when(g > 0)
        def _():
            to_right.wait_recv()

        @pl.when(g == 0)
        def _():
            dst[0] = jnp.zeros(dst.shape[1:], dst.dtype)

        @pl.when(g < groups - 1)
        def _():
            to_left.wait_recv()

        @pl.when(g == groups - 1)
        def _():
            dst[1] = jnp.zeros(dst.shape[1:], dst.dtype)

    def halo_end(kind, src, dst):
        to_left, to_right = halo_copies(kind, src, dst)

        @pl.when(g > 0)
        def _():
            to_left.wait_send()

        @pl.when(g < groups - 1)
        def _():
            to_right.wait_send()

    def near_start(kind, src, dst, by_slide):
        copies = []
        for ds in range(slides):
            for dn in range(near):
                o = ds * near + dn
                s2, n2 = lax.rem(s + ds, slides), lax.rem(n + dn, near)
                part = src.at[s2] if by_slide else src.at[n2]
                if o == 0:
                    dst[0] = part[...]
                else:
                    copies.append(
                        send(part, dst.at[o], near_ss.at[kind, o], near_rs.at[kind, o],
                             (s2, f * near + n2))
                    )
        pending.extend(copies)
        return copies

    def far_start(which, part):
        cube = part.reshape(far, rb, cw)
        far_own[...] = cube
        far_send[which] = cube.astype(far_send.dtype)
        copies = []
        for df in range(1, far):
            f2 = lax.rem(f + df, far)
            copies.append(
                send(far_send.at[which, f2], far_recv.at[which, df], far_ss.at[which, df],
                     far_rs.at[which, df], (s, f2 * near + n))
            )
        pending.extend(copies)
        return far_own[f], copies

    def far_end(own, copies, which):
        total = own
        for df, copy in enumerate(copies, 1):
            copy.wait_recv()
            total = total + far_recv[which, df].astype(F32)
        return total

    def near_product(a, b):
        return mm_tn(a[...].reshape(-1, a.shape[2]), b[...].reshape(-1, b.shape[2]))

    vis_row = vis[...]
    t_col = g * tiles + iota((tiles, 1), 0)

    def is_visible(ids):
        return jnp.sum(jnp.where(vis_row == ids, 1.0, 0.0), axis=1, keepdims=True)

    rank = jnp.sum(jnp.where(vis_row < t_col, 1.0, 0.0), axis=1, keepdims=True).astype(I32)
    here = is_visible(t_col)
    slot = jnp.bitwise_and(rank, groups - 1) * CAP + jnp.bitwise_and(
        jnp.right_shift(rank, log_g), CAP - 1
    )
    by_tile = one_hot(jnp.where(here > 0.5, slot, -1), groups * CAP)
    sbuf[0] = pack(mm_tn(by_tile, emb[0]), groups)

    pl.semaphore_wait(barrier, met)
    first = all_to_all_start(0)
    halo_start(0, og.at[0], og_halo)

    rank_row = iota((tokens, vis_all), 1)
    mine = rank_row == iota((tokens, vis_all), 0) * groups + g
    token_tile = jnp.sum(
        jnp.where(mine, vis_row.astype(F32), 0.0), axis=1, keepdims=True
    ).astype(I32)
    source = jnp.right_shift(token_tile, tiles.bit_length() - 1)
    by_token = one_hot(
        source * CAP + jnp.bitwise_and(iota((tokens, 1), 0), CAP - 1), groups * CAP
    )
    grad_out = og[0]
    for k in range(slides):
        dec_b_send[k] = grad_out[:, k * cw : (k + 1) * cw]
    dctx_mid = mm_nt(grad_out, dec_out[...]).astype(BF)
    new = iota((1, width), 1)
    span = far * rb
    low = jnp.bitwise_and(new, span - 1)
    old = (
        jnp.right_shift(low, rb.bit_length() - 1) * near
        + jnp.right_shift(new, span.bit_length() - 1)
    ) * rb + jnp.bitwise_and(low, rb - 1)
    shuffle = jnp.where(iota((width, width), 0) == old, 1.0, 0.0).astype(BF)

    def near_columns(values, dst):
        moved = mm(values, shuffle).astype(BF)
        for k in range(near):
            dst[k] = moved[:, k * span : (k + 1) * span]

    slots = all_to_all_wait(0)
    dec_b_copies = near_start(0, dec_b_send, dec_b, True)

    tok = mm(by_token, slots)
    tok_r = norm_scale(tok)
    proj = mm((tok * tok_r).astype(BF), enc_qkv[...]).astype(BF)
    q, k, v = proj[:, :width], proj[:, width : 2 * width], proj[:, 2 * width :]
    head_width = width // HEADS
    scale = 1.0 / math.sqrt(head_width)
    rows = HEADS * tokens
    heads = jnp.where(
        jnp.right_shift(iota((rows, width), 0), tokens.bit_length() - 1)
        == jnp.right_shift(iota((rows, width), 1), head_width.bit_length() - 1),
        1.0, 0.0,
    )
    heads_b = heads.astype(BF)

    def spread(values):
        return jnp.concatenate([values] * HEADS, axis=0) * heads_b

    def gather_heads(values):
        return jnp.sum((values * heads).reshape(HEADS, tokens, width), axis=0)

    qx = spread(q)
    logits = mm_nt(qx, k) * scale
    weights = jnp.exp(logits - jnp.max(logits, axis=-1, keepdims=True))
    enc_p = weights / jnp.sum(weights, axis=-1, keepdims=True)
    enc_pb = enc_p.astype(BF)
    enc_ctx = gather_heads(mm(enc_pb, v)).astype(BF)
    encoded = (tok + mm(enc_ctx, enc_out[...])).astype(BF)
    sbuf[1] = pack(mm_tn(by_token, encoded), groups)
    all_to_all_start(1)

    w_mid = win[:, pl.ds(pl.multiple_of(g * tiles, tiles), tiles)]
    w_low = win[:, pl.ds(pl.multiple_of(jnp.maximum(g - 1, 0) * tiles, tiles), tiles)]
    w_high = win[:, pl.ds(pl.multiple_of(jnp.minimum(g + 1, groups - 1) * tiles, tiles), tiles)]
    w_low = jnp.where(g > 0, w_low, -2)
    w_high = jnp.where(g < groups - 1, w_high, -2)
    first_w, last_w = w_mid[:, :1], w_mid[:, tiles - 1 :]
    w_a = jnp.where((w_mid == first_w) | (w_low == first_w), first_w, -1)
    w_b = jnp.where((w_mid == last_w) | (w_high == last_w), last_w, -1)
    mid_columns = as_columns(w_mid)
    in_a = mid_columns[:, :1] == first_w
    in_b = mid_columns[:, :1] == last_w
    vis_low = is_visible(t_col - tiles)
    vis_high = is_visible(t_col + tiles)
    blank = mask_token[...]
    enc_ctx_cols = near_columns(enc_ctx, enc_a_send)
    halo_wait(0, og.at[0], og_halo)
    dctx_low = mm_nt(og_halo[0], dec_out[...])
    dctx_high = mm_nt(og_halo[1], dec_out[...])
    dctx_a = jnp.where(in_a, dctx_mid.astype(F32), dctx_low).astype(BF)
    dctx_b = jnp.where(in_b, dctx_mid.astype(F32), dctx_high).astype(BF)
    lane = iota((1, 2 * head_width), 1)
    half0 = jnp.where(lane < head_width, 1.0, 0.0).astype(BF)
    half1 = jnp.where(lane < head_width, 0.0, 1.0).astype(BF)
    low_half = iota((tiles, 2 * head_width), 1) < head_width

    def same_window(row):
        same = jnp.where(as_columns(row) == row, 1.0, 0.0)
        return jnp.concatenate([same, same], axis=0) > 0.5

    def window_block(qkv, dctx, row, keep):
        allowed = same_window(row)
        for pair in range(HEADS // 2):
            at = slice(pair * 2 * head_width, (pair + 1) * 2 * head_width)
            qs, ks, vs = qkv[0][:, at], qkv[1][:, at], qkv[2][:, at]
            do = dctx[:, at]
            qx = jnp.concatenate([qs * half0, qs * half1], axis=0)
            dox = jnp.concatenate([do * half0, do * half1], axis=0)
            scores = jnp.where(allowed, mm_nt(qx, ks) * scale, NEG)
            e = jnp.exp(scores - jnp.max(scores, axis=-1, keepdims=True))
            p = e / jnp.sum(e, axis=-1, keepdims=True)
            pb = p.astype(BF)
            dp = mm_nt(dox, vs).astype(BF).astype(F32)
            dsb = (p * (dp - jnp.sum(p * dp, axis=-1, keepdims=True)) * scale).astype(BF)
            o = mm(pb, vs)
            dq = mm(dsb, ks)
            results = (
                jnp.where(low_half, dq[:tiles], dq[tiles:]),
                mm_tn(dsb, qx),
                mm_tn(pb, dox),
                jnp.where(low_half, o[:tiles], o[tiles:]),
            )
            for i, value in enumerate(results):
                cols = slice(i * width + at.start, i * width + at.stop)
                if keep is not None:
                    value = jnp.where(keep, value, acc[:, cols])
                acc[:, cols] = value

    def dec_project(values, shown):
        x = jnp.where(shown > 0.5, values.astype(F32), blank)
        r = norm_scale(x)
        out = mm((x * r).astype(BF), dec_qkv[...])
        return x, r, out

    def split3(values):
        values = values.astype(BF)
        return values[:, :width], values[:, width : 2 * width], values[:, 2 * width :]

    slots = all_to_all_wait(1)
    placed = mm(by_tile, slots).astype(BF)
    h_send[...] = placed
    halo_start(1, h_send, h_halo)
    x_mid, r_mid, qkv_mid = dec_project(placed, here)
    window_block(split3(qkv_mid), dctx_mid, w_mid, None)
    halo_wait(1, h_send, h_halo)
    _, _, qkv_low = dec_project(h_halo[0], vis_low)
    window_block(split3(jnp.where(in_a, qkv_mid, qkv_low)), dctx_a, w_a, in_a)
    _, _, qkv_high = dec_project(h_halo[1], vis_high)
    window_block(split3(jnp.where(in_b, qkv_mid, qkv_high)), dctx_b, w_b, in_b)

    near_columns(acc[:, 3 * width :].astype(BF), dec_a_send)
    dec_a_copies = near_start(1, dec_a_send, dec_a, False)
    dnormed = mm_nt(acc[:, : 3 * width].astype(BF), dec_qkv[...])
    dinputs = norm_back(x_mid, r_mid, dnormed) + grad_out.astype(F32)
    sbuf[2] = pack(mm_tn(by_tile, dinputs.astype(BF)), groups)
    all_to_all_start(2)

    for copy in dec_a_copies + dec_b_copies:
        copy.wait_recv()
    dec_own, dec_far = far_start(0, near_product(dec_a, dec_b))

    grad_enc = mm(by_token, all_to_all_wait(2))
    grad_enc_b = grad_enc.astype(BF)
    for j in range(slides):
        enc_b_send[j] = grad_enc_b[:, j * cw : (j + 1) * cw]
    enc_copies = near_start(2, enc_a_send, enc_a, False) + near_start(3, enc_b_send, enc_b, True)
    dox = spread(mm_nt(grad_enc_b, enc_out[...]).astype(BF))
    dp = mm_nt(dox, v).astype(BF).astype(F32)
    dsb = (enc_p * (dp - jnp.sum(enc_p * dp, axis=-1, keepdims=True)) * scale).astype(BF)
    dq = gather_heads(mm(dsb, k))
    dk = mm_tn(dsb, qx)
    dv = mm_tn(enc_pb, dox)
    dproj = jnp.concatenate([dq, dk, dv], axis=1).astype(BF)
    dn = mm_nt(dproj, enc_qkv[...]).astype(BF).astype(F32)
    dtok = (norm_back(tok, tok_r, dn) + grad_enc).astype(BF)
    sbuf[3] = pack(mm_tn(by_token, dtok), groups)
    all_to_all_start(3)

    out_dec[...] = far_end(dec_own, dec_far, 0)
    for copy in enc_copies:
        copy.wait_recv()
    enc_own, enc_far = far_start(1, near_product(enc_a, enc_b))
    out_tiles[0] = mm(by_tile, all_to_all_wait(3)).astype(BF)
    out_enc[...] = far_end(enc_own, enc_far, 1)
    for copy in pending:
        copy.wait_send()
    halo_end(0, og.at[0], og_halo)
    halo_end(1, h_send, h_halo)


def shards(groups, slides, emb, vis, win, og, mask_token, enc_qkv, enc_out, dec_qkv, dec_out):
    _, tiles, width = emb.shape
    tokens = vis.shape[1] // groups
    near = min(4, groups)
    far = groups // near
    rb, cw = width // groups, width // slides
    span = far * rb
    ns = near * slides
    far_type = BF if rb % 16 == 0 else F32
    dma = pltpu.SemaphoreType.DMA
    vmem = pl.BlockSpec(memory_space=pltpu.VMEM)
    return pl.pallas_call(
        functools.partial(kernel, groups, slides, near),
        out_shape=(
            jax.ShapeDtypeStruct(emb.shape, BF),
            jax.ShapeDtypeStruct((rb, cw), F32),
            jax.ShapeDtypeStruct((rb, cw), F32),
        ),
        in_specs=[vmem] * 9,
        out_specs=(vmem,) * 3,
        scratch_shapes=[
            pltpu.VMEM((4, groups, 2 * CAP, width // 2), BF),
            pltpu.VMEM((4, groups, 2 * CAP, width // 2), BF),
            pltpu.VMEM((2, tiles, width), BF),
            pltpu.VMEM((tiles, width), BF),
            pltpu.VMEM((2, tiles, width), BF),
            pltpu.VMEM((near, tiles, span), BF),
            pltpu.VMEM((slides, tiles, cw), BF),
            pltpu.VMEM((ns, tiles, span), BF),
            pltpu.VMEM((ns, tiles, cw), BF),
            pltpu.VMEM((near, tokens, span), BF),
            pltpu.VMEM((slides, tokens, cw), BF),
            pltpu.VMEM((ns, tokens, span), BF),
            pltpu.VMEM((ns, tokens, cw), BF),
            pltpu.VMEM((2, far, rb, cw), far_type),
            pltpu.VMEM((2, far, rb, cw), far_type),
            pltpu.VMEM((far, rb, cw), F32),
            pltpu.VMEM((tiles, 4 * width), F32),
            dma((4, groups)), dma((4, groups)),
            dma((2, 2)), dma((2, 2)),
            dma((4, ns)), dma((4, ns)),
            dma((2, far)), dma((2, far)),
        ],
        compiler_params=pltpu.CompilerParams(
            collective_id=0, has_side_effects=True, vmem_limit_bytes=44 * 1024 * 1024
        ),
    )(emb, vis, win, og, mask_token[None, :], enc_qkv, enc_out, dec_qkv, dec_out)


def solution(mesh):
    placed = (
        P("slide", "grid", None),
        P("slide", None),
        P("slide", None),
        P("slide", "grid", None),
        P(),
        P(),
        P(),
        P(),
        P(),
    )
    return jax.shard_map(
        functools.partial(shards, mesh.shape["grid"], mesh.shape["slide"]),
        mesh=mesh,
        in_specs=placed,
        out_specs=(P("slide", "grid", None), P("grid", "slide"), P("grid", "slide")),
        check_vma=False,
    )
```

```python
import functools
import math

import jax
import jax.numpy as jnp
from jax import lax
from jax.experimental import pallas as pl
from jax.experimental.pallas import tpu as pltpu
from jax.sharding import PartitionSpec as P

HEADS = 8
EPS = 1e-06
CAP = 8
NEG = -1e30
BF = jnp.bfloat16
F32 = jnp.float32
I32 = jnp.int32
MESH = pl.DeviceIdType.MESH


def mm(a, b):
    return lax.dot_general(a, b, (((1,), (0,)), ((), ())), preferred_element_type=F32)


def mm_nt(a, b):
    return lax.dot_general(a, b, (((1,), (1,)), ((), ())), preferred_element_type=F32)


def mm_tn(a, b):
    return lax.dot_general(a, b, (((0,), (0,)), ((), ())), preferred_element_type=F32)


def iota(shape, dim):
    return lax.broadcasted_iota(I32, shape, dim)


def norm_scale(x):
    return lax.rsqrt(jnp.mean(x * x, axis=-1, keepdims=True) + EPS)


def norm_back(x, r, dn):
    return r * dn - x * (r * r * r * jnp.mean(dn * x, axis=-1, keepdims=True))


def pack(rows, peers):
    width = rows.shape[1]
    cube = rows.reshape(peers, CAP, width)
    halves = [cube[:, :, : width // 2], cube[:, :, width // 2 :]]
    return jnp.concatenate(halves, axis=1).astype(BF)


def unpack(cube):
    peers, rows, half = cube.shape
    wide = cube.astype(F32)
    wide = jnp.concatenate([wide[:, :CAP], wide[:, CAP:]], axis=2)
    return wide.reshape(peers * CAP, 2 * half).astype(BF)


def one_hot(ids, count):
    return jnp.where(iota((ids.shape[0], count), 1) == ids, 1.0, 0.0).astype(BF)


def as_columns(row):
    n = row.shape[1]
    return jnp.broadcast_to(row, (n, n)).T


def kernel(
    groups, slides, near,
    emb_in, vis_in, win_in, og_in, mask_in, enc_qkv_in, enc_out_in, dec_qkv_in, dec_out_in,
    out_tiles, out_enc, out_dec,
    emb, vis, win, og, mask_token, enc_qkv, enc_out, dec_qkv, dec_out,
    sbuf, rbuf, og_halo, h_send, h_halo,
    dec_a_send, dec_b_send, dec_a, dec_b,
    enc_a_send, enc_b_send, enc_a, enc_b,
    far_send, far_recv, far_own, acc_q, acc_kv, acc_o, load_s,
    a2a_ss, a2a_rs, halo_ss, halo_rs, near_ss, near_rs, far_ss, far_rs,
):
    s = lax.axis_index("slide")
    g = lax.axis_index("grid")
    tiles, width = emb.shape
    vis_all = vis.shape[1]
    tokens = vis_all // groups
    far = groups // near
    rb, cw = out_enc.shape
    n = lax.rem(g, near)
    f = lax.div(g, near)
    log_g = groups.bit_length() - 1
    pending = []
    loads = []
    for i, (src, dst) in enumerate((
        (vis_in, vis), (emb_in.at[0], emb), (og_in.at[0], og), (enc_qkv_in, enc_qkv),
        (dec_out_in, dec_out), (win_in, win), (enc_out_in, enc_out), (mask_in, mask_token),
        (dec_qkv_in, dec_qkv),
    )):
        loads.append((dst, pltpu.make_async_copy(src, dst, load_s.at[i])))
        loads[i][1].start()

    def loaded(*refs):
        for dst, copy in loads:
            if any(dst is ref for ref in refs):
                copy.wait()

    barrier = pltpu.get_barrier_semaphore()
    met = 0
    for j in range(1, groups):
        pl.semaphore_signal(
            barrier, inc=1, device_id=(s, lax.rem(g + j, groups)), device_id_type=MESH
        )
        met += 1
    for ds in range(1, slides):
        for dn in range(near):
            peer = (lax.rem(s + ds, slides), f * near + lax.rem(n + dn, near))
            pl.semaphore_signal(barrier, inc=1, device_id=peer, device_id_type=MESH)
            met += 1

    def send(src, dst, ss, rs, peer):
        copy = pltpu.make_async_remote_copy(
            src_ref=src, dst_ref=dst, send_sem=ss, recv_sem=rs,
            device_id=peer, device_id_type=MESH,
        )
        copy.start()
        return copy

    def all_to_all_start(stage):
        copies = []
        for j in sorted(range(1, groups), key=lambda j: -min(j, groups - j)):
            dst = lax.rem(g + j, groups)
            copies.append(
                send(sbuf.at[stage, dst], rbuf.at[stage, g], a2a_ss.at[stage, j],
                     a2a_rs.at[stage, j], (s, dst))
            )
        rbuf[stage, g] = sbuf[stage, g]
        pending.extend(copies)
        return copies

    def all_to_all_wait(stage):
        for j in range(1, groups):
            src = lax.rem(g + groups - j, groups)
            pltpu.make_async_remote_copy(
                src_ref=sbuf.at[stage, src], dst_ref=rbuf.at[stage, src],
                send_sem=a2a_ss.at[stage, j], recv_sem=a2a_rs.at[stage, j],
                device_id=(s, src), device_id_type=MESH,
            ).wait_recv()
        return unpack(rbuf[stage])

    def halo_copies(kind, src, dst):
        left = jnp.maximum(g - 1, 0)
        right = jnp.minimum(g + 1, groups - 1)

        def to(side, peer):
            return pltpu.make_async_remote_copy(
                src_ref=src, dst_ref=dst.at[side], send_sem=halo_ss.at[kind, side],
                recv_sem=halo_rs.at[kind, side], device_id=(s, peer), device_id_type=MESH,
            )

        return to(1, left), to(0, right)

    def halo_start(kind, src, dst):
        to_left, to_right = halo_copies(kind, src, dst)

        @pl.when(g > 0)
        def _():
            to_left.start()

        @pl.when(g < groups - 1)
        def _():
            to_right.start()

    def halo_wait(kind, src, dst):
        to_left, to_right = halo_copies(kind, src, dst)

        @pl.when(g > 0)
        def _():
            to_right.wait_recv()

        @pl.when(g == 0)
        def _():
            dst[0] = jnp.zeros(dst.shape[1:], dst.dtype)

        @pl.when(g < groups - 1)
        def _():
            to_left.wait_recv()

        @pl.when(g == groups - 1)
        def _():
            dst[1] = jnp.zeros(dst.shape[1:], dst.dtype)

    def halo_end(kind, src, dst):
        to_left, to_right = halo_copies(kind, src, dst)

        @pl.when(g > 0)
        def _():
            to_left.wait_send()

        @pl.when(g < groups - 1)
        def _():
            to_right.wait_send()

    def near_start(kind, src, dst, by_slide):
        copies = []
        for ds in range(slides):
            for dn in range(near):
                o = ds * near + dn
                s2, n2 = lax.rem(s + ds, slides), lax.rem(n + dn, near)
                part = src.at[s2] if by_slide else src.at[n2]
                if o == 0:
                    dst[0] = part[...]
                else:
                    copies.append(
                        send(part, dst.at[o], near_ss.at[kind, o], near_rs.at[kind, o],
                             (s2, f * near + n2))
                    )
        pending.extend(copies)
        return copies

    def far_start(which, part):
        cube = part.reshape(far, rb, cw)
        far_own[...] = cube
        far_send[which] = cube.astype(far_send.dtype)
        copies = []
        for df in range(1, far):
            f2 = lax.rem(f + df, far)
            copies.append(
                send(far_send.at[which, f2], far_recv.at[which, df], far_ss.at[which, df],
                     far_rs.at[which, df], (s, f2 * near + n))
            )
        pending.extend(copies)
        return far_own[f], copies

    def far_end(own, copies, which):
        total = own
        for df, copy in enumerate(copies, 1):
            copy.wait_recv()
            total = total + far_recv[which, df].astype(F32)
        return total

    def near_product(a, b):
        return mm_tn(a[...].reshape(-1, a.shape[2]), b[...].reshape(-1, b.shape[2]))

    loaded(vis)
    vis_row = vis[...]
    t_col = g * tiles + iota((tiles, 1), 0)

    def is_visible(ids):
        return jnp.sum(jnp.where(vis_row == ids, 1.0, 0.0), axis=1, keepdims=True)

    rank = jnp.sum(jnp.where(vis_row < t_col, 1.0, 0.0), axis=1, keepdims=True).astype(I32)
    here = is_visible(t_col)
    slot = jnp.bitwise_and(rank, groups - 1) * CAP + jnp.bitwise_and(
        jnp.right_shift(rank, log_g), CAP - 1
    )
    by_tile = one_hot(jnp.where(here > 0.5, slot, -1), groups * CAP)
    loaded(emb)
    sbuf[0] = pack(mm_tn(by_tile, emb[...]), groups)

    pl.semaphore_wait(barrier, met)
    all_to_all_start(0)
    loaded(og)
    halo_start(0, og, og_halo)

    rank_row = iota((tokens, vis_all), 1)
    mine = rank_row == iota((tokens, vis_all), 0) * groups + g
    token_tile = jnp.sum(
        jnp.where(mine, vis_row.astype(F32), 0.0), axis=1, keepdims=True
    ).astype(I32)
    source = jnp.right_shift(token_tile, tiles.bit_length() - 1)
    by_token = one_hot(
        source * CAP + jnp.bitwise_and(iota((tokens, 1), 0), CAP - 1), groups * CAP
    )
    grad_out = og[...]
    for k in range(slides):
        dec_b_send[k] = grad_out[:, k * cw : (k + 1) * cw]
    loaded(dec_out)
    dctx_mid = mm_nt(grad_out, dec_out[...]).astype(BF)
    new = iota((1, width), 1)
    span = far * rb
    low = jnp.bitwise_and(new, span - 1)
    old = (
        jnp.right_shift(low, rb.bit_length() - 1) * near
        + jnp.right_shift(new, span.bit_length() - 1)
    ) * rb + jnp.bitwise_and(low, rb - 1)
    shuffle = jnp.where(iota((width, width), 0) == old, 1.0, 0.0).astype(BF)

    def near_columns(values, dst, product=mm):
        moved = product(values, shuffle).astype(BF)
        for k in range(near):
            dst[k] = moved[:, k * span : (k + 1) * span]

    loaded(enc_qkv, enc_out, win, mask_token, dec_qkv)
    slots = all_to_all_wait(0)

    tok = mm(by_token, slots)
    tok_r = norm_scale(tok)
    proj = mm((tok * tok_r).astype(BF), enc_qkv[...]).astype(BF)
    q, k, v = proj[:, :width], proj[:, width : 2 * width], proj[:, 2 * width :]
    head_width = width // HEADS
    scale = 1.0 / math.sqrt(head_width)
    rows = HEADS * tokens
    heads = jnp.where(
        jnp.right_shift(iota((rows, width), 0), tokens.bit_length() - 1)
        == jnp.right_shift(iota((rows, width), 1), head_width.bit_length() - 1),
        1.0, 0.0,
    )
    heads_b = heads.astype(BF)

    def spread(values):
        return jnp.concatenate([values] * HEADS, axis=0) * heads_b

    def gather_heads(values):
        return jnp.sum((values * heads).reshape(HEADS, tokens, width), axis=0)

    qx = spread(q)
    logits = mm_nt(k, qx) * scale
    weights = jnp.exp(logits - jnp.max(logits, axis=0, keepdims=True))
    enc_p = weights / jnp.sum(weights, axis=0, keepdims=True)
    enc_pb = enc_p.astype(BF)
    enc_ctx = gather_heads(mm_tn(enc_pb, v)).astype(BF)
    encoded = (tok + mm(enc_ctx, enc_out[...])).astype(BF)
    sbuf[1] = pack(mm_tn(by_token, encoded), groups)
    all_to_all_start(1)

    w_mid = win[:, pl.ds(pl.multiple_of(g * tiles, tiles), tiles)]
    w_low = win[:, pl.ds(pl.multiple_of(jnp.maximum(g - 1, 0) * tiles, tiles), tiles)]
    w_high = win[:, pl.ds(pl.multiple_of(jnp.minimum(g + 1, groups - 1) * tiles, tiles), tiles)]
    w_low = jnp.where(g > 0, w_low, -2)
    w_high = jnp.where(g < groups - 1, w_high, -2)
    first_w, last_w = w_mid[:, :1], w_mid[:, tiles - 1 :]
    w_a = jnp.where((w_mid == first_w) | (w_low == first_w), first_w, -1)
    w_b = jnp.where((w_mid == last_w) | (w_high == last_w), last_w, -1)
    mid_columns = as_columns(w_mid)
    in_a = mid_columns[:, :1] == first_w
    in_b = mid_columns[:, :1] == last_w
    vis_low = is_visible(t_col - tiles)
    vis_high = is_visible(t_col + tiles)
    blank = mask_token[...]
    near_columns(enc_ctx, enc_a_send)
    halo_wait(0, og, og_halo)
    dctx_low = mm_nt(og_halo[0], dec_out[...])
    dctx_high = mm_nt(og_halo[1], dec_out[...])
    dctx_a = jnp.where(in_a, dctx_mid.astype(F32), dctx_low).astype(BF)
    dctx_b = jnp.where(in_b, dctx_mid.astype(F32), dctx_high).astype(BF)
    lane = iota((1, 2 * head_width), 1)
    half0 = jnp.where(lane < head_width, 1.0, 0.0).astype(BF)
    half1 = jnp.where(lane < head_width, 0.0, 1.0).astype(BF)
    scaled0, scaled1 = half0 * BF(scale), half1 * BF(scale)
    at_a, at_b = w_mid == first_w, w_mid == last_w

    def same_window(row):
        same = jnp.where(as_columns(row) == row, 0.0, NEG)
        return jnp.concatenate([same, same], axis=1)

    def diagonal(values):
        return jnp.concatenate(
            [values[:head_width, :tiles], values[head_width:, tiles:]], axis=0
        )

    def window_block(qkv, dctx, row, keep_rows, keep_lanes):
        bias = same_window(row)
        for pair in range(HEADS // 2):
            at = slice(pair * 2 * head_width, (pair + 1) * 2 * head_width)
            qs, ks, vs = qkv[0][:, at], qkv[1][:, at], qkv[2][:, at]
            do = dctx[:, at]
            qx = jnp.concatenate([qs * scaled0, qs * scaled1], axis=0)
            dox = jnp.concatenate([do * half0, do * half1], axis=0)
            scores = mm_nt(ks, qx) + bias
            e = jnp.exp(scores - jnp.max(scores, axis=0, keepdims=True))
            p = e * (1.0 / jnp.sum(e, axis=0, keepdims=True))
            pb = p.astype(BF)
            dp = mm_nt(vs, dox)
            dsb = (p * (dp - jnp.sum(p * dp, axis=0, keepdims=True))).astype(BF)
            o = diagonal(mm_tn(vs, pb))
            dq = diagonal(mm_tn(ks, dsb))
            dk = mm(dsb, qx)
            dv = mm(pb, dox)
            at_v = slice(width + at.start, width + at.stop)
            if keep_rows is not None:
                o = jnp.where(keep_lanes, o, acc_o[at])
                dq = jnp.where(keep_lanes, dq, acc_q[at])
                dk = jnp.where(keep_rows, dk, acc_kv[:, at])
                dv = jnp.where(keep_rows, dv, acc_kv[:, at_v])
            acc_o[at] = o
            acc_q[at] = dq
            acc_kv[:, at] = dk
            acc_kv[:, at_v] = dv

    def dec_project(values, shown):
        x = jnp.where(shown > 0.5, values.astype(F32), blank)
        r = norm_scale(x)
        out = mm((x * r).astype(BF), dec_qkv[...])
        return x, r, out

    def split3(values):
        values = values.astype(BF)
        return values[:, :width], values[:, width : 2 * width], values[:, 2 * width :]

    slots = all_to_all_wait(1)
    placed = mm(by_tile, slots).astype(BF)
    h_send[...] = placed
    halo_start(1, h_send, h_halo)
    x_mid, r_mid, qkv_mid = dec_project(placed, here)
    dec_b_copies = near_start(0, dec_b_send, dec_b, True)
    window_block(split3(qkv_mid), dctx_mid, w_mid, None, None)
    halo_wait(1, h_send, h_halo)
    _, _, qkv_edge = dec_project(
        h_halo[...].reshape(2 * tiles, width), jnp.concatenate([vis_low, vis_high], axis=0)
    )
    qkv_a = jnp.where(in_a, qkv_mid, qkv_edge[:tiles])
    qkv_b = jnp.where(in_b, qkv_mid, qkv_edge[tiles:])
    window_block(split3(qkv_a), dctx_a, w_a, in_a, at_a)
    window_block(split3(qkv_b), dctx_b, w_b, in_b, at_b)

    grad_q = (acc_q[...].T * scale).astype(BF)
    dnormed = mm_nt(grad_q, dec_qkv[:, :width]) + mm_nt(
        acc_kv[...].astype(BF), dec_qkv[:, width:]
    )
    dinputs = norm_back(x_mid, r_mid, dnormed) + grad_out.astype(F32)
    sbuf[2] = pack(mm_tn(by_tile, dinputs.astype(BF)), groups)
    all_to_all_start(2)

    near_columns(acc_o[...].astype(BF), dec_a_send, mm_tn)
    dec_a_copies = near_start(1, dec_a_send, dec_a, False)
    for copy in dec_a_copies + dec_b_copies:
        copy.wait_recv()
    dec_own, dec_far = far_start(0, near_product(dec_a, dec_b))

    grad_enc = mm(by_token, all_to_all_wait(2))
    grad_enc_b = grad_enc.astype(BF)
    for j in range(slides):
        enc_b_send[j] = grad_enc_b[:, j * cw : (j + 1) * cw]
    enc_copies = near_start(2, enc_a_send, enc_a, False) + near_start(3, enc_b_send, enc_b, True)
    dox = spread(mm_nt(grad_enc_b, enc_out[...]).astype(BF))
    dp = mm_nt(v, dox)
    dsb = (enc_p * (dp - jnp.sum(enc_p * dp, axis=0, keepdims=True)) * scale).astype(BF)
    dq = gather_heads(mm_tn(dsb, k))
    dk = mm(dsb, qx)
    dv = mm(enc_pb, dox)
    dproj = jnp.concatenate([dq, dk, dv], axis=1).astype(BF)
    dn = mm_nt(dproj, enc_qkv[...]).astype(BF).astype(F32)
    dtok = (norm_back(tok, tok_r, dn) + grad_enc).astype(BF)
    sbuf[3] = pack(mm_tn(by_token, dtok), groups)
    all_to_all_start(3)

    out_dec[...] = far_end(dec_own, dec_far, 0)
    for copy in enc_copies:
        copy.wait_recv()
    enc_own, enc_far = far_start(1, near_product(enc_a, enc_b))
    out_tiles[0] = mm(by_tile, all_to_all_wait(3)).astype(BF)
    out_enc[...] = far_end(enc_own, enc_far, 1)
    for copy in pending:
        copy.wait_send()
    halo_end(0, og, og_halo)
    halo_end(1, h_send, h_halo)


def shards(groups, slides, emb, vis, win, og, mask_token, enc_qkv, enc_out, dec_qkv, dec_out):
    _, tiles, width = emb.shape
    tokens = vis.shape[1] // groups
    near = min(4, groups)
    far = groups // near
    rb, cw = width // groups, width // slides
    span = far * rb
    ns = near * slides
    far_type = BF if rb % 16 == 0 else F32
    dma = pltpu.SemaphoreType.DMA
    vmem = pl.BlockSpec(memory_space=pltpu.VMEM)
    return pl.pallas_call(
        functools.partial(kernel, groups, slides, near),
        out_shape=(
            jax.ShapeDtypeStruct(emb.shape, BF),
            jax.ShapeDtypeStruct((rb, cw), F32),
            jax.ShapeDtypeStruct((rb, cw), F32),
        ),
        in_specs=[pl.BlockSpec(memory_space=pl.ANY)] * 9,
        out_specs=(vmem,) * 3,
        scratch_shapes=[
            pltpu.VMEM((tiles, width), BF),
            pltpu.VMEM(vis.shape, I32),
            pltpu.VMEM(win.shape, I32),
            pltpu.VMEM((tiles, width), BF),
            pltpu.VMEM((1, width), F32),
            pltpu.VMEM(enc_qkv.shape, BF),
            pltpu.VMEM(enc_out.shape, BF),
            pltpu.VMEM(dec_qkv.shape, BF),
            pltpu.VMEM(dec_out.shape, BF),
            pltpu.VMEM((4, groups, 2 * CAP, width // 2), BF),
            pltpu.VMEM((4, groups, 2 * CAP, width // 2), BF),
            pltpu.VMEM((2, tiles, width), BF),
            pltpu.VMEM((tiles, width), BF),
            pltpu.VMEM((2, tiles, width), BF),
            pltpu.VMEM((near, tiles, span), BF),
            pltpu.VMEM((slides, tiles, cw), BF),
            pltpu.VMEM((ns, tiles, span), BF),
            pltpu.VMEM((ns, tiles, cw), BF),
            pltpu.VMEM((near, tokens, span), BF),
            pltpu.VMEM((slides, tokens, cw), BF),
            pltpu.VMEM((ns, tokens, span), BF),
            pltpu.VMEM((ns, tokens, cw), BF),
            pltpu.VMEM((2, far, rb, cw), far_type),
            pltpu.VMEM((2, far, rb, cw), far_type),
            pltpu.VMEM((far, rb, cw), F32),
            pltpu.VMEM((width, tiles), F32),
            pltpu.VMEM((tiles, 2 * width), F32),
            pltpu.VMEM((width, tiles), F32),
            dma((9,)),
            dma((4, groups)), dma((4, groups)),
            dma((2, 2)), dma((2, 2)),
            dma((4, ns)), dma((4, ns)),
            dma((2, far)), dma((2, far)),
        ],
        compiler_params=pltpu.CompilerParams(
            collective_id=0, has_side_effects=True, vmem_limit_bytes=60 * 1024 * 1024
        ),
    )(emb, vis, win, og, mask_token[None, :], enc_qkv, enc_out, dec_qkv, dec_out)


def solution(mesh):
    placed = (
        P("slide", "grid", None),
        P("slide", None),
        P("slide", None),
        P("slide", "grid", None),
        P(),
        P(),
        P(),
        P(),
        P(),
    )
    return jax.shard_map(
        functools.partial(shards, mesh.shape["grid"], mesh.shape["slide"]),
        mesh=mesh,
        in_specs=placed,
        out_specs=(P("slide", "grid", None), P("grid", "slide"), P("grid", "slide")),
        check_vma=False,
    )
```

```python
import functools
import math

import jax
import jax.numpy as jnp
from jax import lax
from jax.experimental import pallas as pl
from jax.experimental.pallas import tpu as pltpu
from jax.sharding import PartitionSpec as P

HEADS = 8
EPS = 1e-06
CAP = 8
NEG = -1e30
BF = jnp.bfloat16
F32 = jnp.float32
I32 = jnp.int32
MESH = pl.DeviceIdType.MESH


def mm(a, b):
    return lax.dot_general(a, b, (((1,), (0,)), ((), ())), preferred_element_type=F32)


def mm_nt(a, b):
    return lax.dot_general(a, b, (((1,), (1,)), ((), ())), preferred_element_type=F32)


def mm_tn(a, b):
    return lax.dot_general(a, b, (((0,), (0,)), ((), ())), preferred_element_type=F32)


def iota(shape, dim):
    return lax.broadcasted_iota(I32, shape, dim)


def norm_scale(x):
    return lax.rsqrt(jnp.mean(x * x, axis=-1, keepdims=True) + EPS)


def norm_back(x, r, dn):
    return r * dn - x * (r * r * r * jnp.mean(dn * x, axis=-1, keepdims=True))


def fold(rows):
    half = rows.shape[1] // 2
    return jnp.concatenate([rows[:, :half], rows[:, half:]], axis=0)


def unfold(rows):
    n = rows.shape[0] // 2
    return jnp.concatenate([rows[:n], rows[n:]], axis=1)


def one_hot(peer, place, count):
    left = peer * (2 * CAP) + place
    ids = jnp.concatenate([left, left + jnp.where(peer < 0, 0, CAP)], axis=0)
    return jnp.where(iota((ids.shape[0], 2 * CAP * count), 1) == ids, 1.0, 0.0).astype(BF)


def as_columns(row):
    n = row.shape[1]
    return jnp.broadcast_to(row, (n, n)).T


def kernel(
    groups, slides, near,
    emb_in, vis_in, win_in, og_in, mask_in, enc_qkv_in, enc_out_in, dec_qkv_in, dec_out_in,
    out_tiles, out_enc, out_dec,
    emb, vis, win, og, mask_token, enc_qkv, enc_out, dec_qkv, dec_out,
    sbuf, rbuf, og_halo, h_send, h_halo,
    dec_a_send, dec_b_send, dec_a, dec_b,
    enc_a_send, enc_b_send, enc_a, enc_b,
    far_send, far_recv, far_own, acc_q, acc_kv, acc_o, load_s,
    a2a_ss, a2a_rs, halo_ss, halo_rs, near_ss, near_rs, far_ss, far_rs,
):
    s = lax.axis_index("slide")
    g = lax.axis_index("grid")
    tiles, width = emb.shape
    vis_all = vis.shape[1]
    tokens = vis_all // groups
    far = groups // near
    rb, cw = out_enc.shape
    n = lax.rem(g, near)
    f = lax.div(g, near)
    log_g = groups.bit_length() - 1
    pending = []
    loads = []
    for i, (src, dst) in enumerate((
        (vis_in, vis), (emb_in.at[0], emb), (og_in.at[0], og), (enc_qkv_in, enc_qkv),
        (dec_out_in, dec_out), (win_in, win), (enc_out_in, enc_out), (mask_in, mask_token),
        (dec_qkv_in, dec_qkv),
    )):
        loads.append((dst, pltpu.make_async_copy(src, dst, load_s.at[i])))
        loads[i][1].start()

    def loaded(*refs):
        for dst, copy in loads:
            if any(dst is ref for ref in refs):
                copy.wait()

    barrier = pltpu.get_barrier_semaphore()
    met = 0
    for j in range(1, groups):
        pl.semaphore_signal(
            barrier, inc=1, device_id=(s, lax.rem(g + j, groups)), device_id_type=MESH
        )
        met += 1
    for ds in range(1, slides):
        for dn in range(near):
            peer = (lax.rem(s + ds, slides), f * near + lax.rem(n + dn, near))
            pl.semaphore_signal(barrier, inc=1, device_id=peer, device_id_type=MESH)
            met += 1

    def send(src, dst, ss, rs, peer):
        copy = pltpu.make_async_remote_copy(
            src_ref=src, dst_ref=dst, send_sem=ss, recv_sem=rs,
            device_id=peer, device_id_type=MESH,
        )
        copy.start()
        return copy

    def all_to_all_start(stage):
        copies = []
        for j in sorted(range(1, groups), key=lambda j: -min(j, groups - j)):
            dst = lax.rem(g + j, groups)
            copies.append(
                send(sbuf.at[stage, dst], rbuf.at[stage, g], a2a_ss.at[stage, j],
                     a2a_rs.at[stage, j], (s, dst))
            )
        rbuf[stage, g] = sbuf[stage, g]
        pending.extend(copies)
        return copies

    def all_to_all_wait(stage):
        for j in range(1, groups):
            src = lax.rem(g + groups - j, groups)
            pltpu.make_async_remote_copy(
                src_ref=sbuf.at[stage, src], dst_ref=rbuf.at[stage, src],
                send_sem=a2a_ss.at[stage, j], recv_sem=a2a_rs.at[stage, j],
                device_id=(s, src), device_id_type=MESH,
            ).wait_recv()
        return rbuf[stage].reshape(groups * 2 * CAP, width // 2)

    def halo_copies(kind, src, dst):
        left = jnp.maximum(g - 1, 0)
        right = jnp.minimum(g + 1, groups - 1)

        def to(side, peer):
            return pltpu.make_async_remote_copy(
                src_ref=src, dst_ref=dst.at[side], send_sem=halo_ss.at[kind, side],
                recv_sem=halo_rs.at[kind, side], device_id=(s, peer), device_id_type=MESH,
            )

        return to(1, left), to(0, right)

    def halo_start(kind, src, dst):
        to_left, to_right = halo_copies(kind, src, dst)

        @pl.when(g > 0)
        def _():
            to_left.start()

        @pl.when(g < groups - 1)
        def _():
            to_right.start()

    def halo_wait(kind, src, dst):
        to_left, to_right = halo_copies(kind, src, dst)

        @pl.when(g > 0)
        def _():
            to_right.wait_recv()

        @pl.when(g == 0)
        def _():
            dst[0] = jnp.zeros(dst.shape[1:], dst.dtype)

        @pl.when(g < groups - 1)
        def _():
            to_left.wait_recv()

        @pl.when(g == groups - 1)
        def _():
            dst[1] = jnp.zeros(dst.shape[1:], dst.dtype)

    def halo_end(kind, src, dst):
        to_left, to_right = halo_copies(kind, src, dst)

        @pl.when(g > 0)
        def _():
            to_left.wait_send()

        @pl.when(g < groups - 1)
        def _():
            to_right.wait_send()

    def near_start(kind, src, dst, by_slide):
        copies = []
        for ds in range(slides):
            for dn in range(near):
                o = ds * near + dn
                s2, n2 = lax.rem(s + ds, slides), lax.rem(n + dn, near)
                part = src.at[s2] if by_slide else src.at[n2]
                if o == 0:
                    dst[0] = part[...]
                else:
                    copies.append(
                        send(part, dst.at[o], near_ss.at[kind, o], near_rs.at[kind, o],
                             (s2, f * near + n2))
                    )
        pending.extend(copies)
        return copies

    def far_start(which, part):
        cube = part.reshape(far, rb, cw)
        far_own[...] = cube
        far_send[which] = cube.astype(far_send.dtype)
        copies = []
        for df in range(1, far):
            f2 = lax.rem(f + df, far)
            copies.append(
                send(far_send.at[which, f2], far_recv.at[which, df], far_ss.at[which, df],
                     far_rs.at[which, df], (s, f2 * near + n))
            )
        pending.extend(copies)
        return far_own[f], copies

    def far_end(own, copies, which):
        total = own
        for df, copy in enumerate(copies, 1):
            copy.wait_recv()
            total = total + far_recv[which, df].astype(F32)
        return total

    def near_product(a, b):
        return mm_tn(a[...].reshape(-1, a.shape[2]), b[...].reshape(-1, b.shape[2]))

    loaded(vis)
    vis_row = vis[...]
    t_col = g * tiles + iota((tiles, 1), 0)

    def is_visible(ids):
        return jnp.sum(jnp.where(vis_row == ids, 1.0, 0.0), axis=1, keepdims=True)

    rank = jnp.sum(jnp.where(vis_row < t_col, 1.0, 0.0), axis=1, keepdims=True).astype(I32)
    here = is_visible(t_col)
    peer = jnp.where(here > 0.5, jnp.bitwise_and(rank, groups - 1), -1)
    place = jnp.bitwise_and(jnp.right_shift(rank, log_g), CAP - 1)
    by_tile = one_hot(peer, place, groups)

    def to_slots(stage, by_row, rows):
        moved = mm_tn(by_row, fold(rows)).astype(BF)
        sbuf[stage] = moved.reshape(groups, 2 * CAP, width // 2)

    def from_slots(by_row, slots):
        return unfold(mm(by_row, slots))

    loaded(emb)
    to_slots(0, by_tile, emb[...])

    pl.semaphore_wait(barrier, met)
    all_to_all_start(0)
    loaded(og)
    halo_start(0, og, og_halo)

    rank_row = iota((tokens, vis_all), 1)
    mine = rank_row == iota((tokens, vis_all), 0) * groups + g
    token_tile = jnp.sum(
        jnp.where(mine, vis_row.astype(F32), 0.0), axis=1, keepdims=True
    ).astype(I32)
    source = jnp.right_shift(token_tile, tiles.bit_length() - 1)
    by_token = one_hot(source, jnp.bitwise_and(iota((tokens, 1), 0), CAP - 1), groups)
    grad_out = og[...]
    for k in range(slides):
        dec_b_send[k] = grad_out[:, k * cw : (k + 1) * cw]
    loaded(dec_out)
    dctx_mid = mm_nt(grad_out, dec_out[...]).astype(BF)
    new = iota((1, width), 1)
    span = far * rb
    low = jnp.bitwise_and(new, span - 1)
    old = (
        jnp.right_shift(low, rb.bit_length() - 1) * near
        + jnp.right_shift(new, span.bit_length() - 1)
    ) * rb + jnp.bitwise_and(low, rb - 1)
    shuffle = jnp.where(iota((width, width), 0) == old, 1.0, 0.0).astype(BF)

    def near_columns(values, dst, product=mm):
        moved = product(values, shuffle).astype(BF)
        for k in range(near):
            dst[k] = moved[:, k * span : (k + 1) * span]

    loaded(enc_qkv, enc_out, win, mask_token, dec_qkv)
    slots = all_to_all_wait(0)

    tok = from_slots(by_token, slots)
    tok_r = norm_scale(tok)
    proj = mm((tok * tok_r).astype(BF), enc_qkv[...]).astype(BF)
    q, k, v = proj[:, :width], proj[:, width : 2 * width], proj[:, 2 * width :]
    head_width = width // HEADS
    scale = 1.0 / math.sqrt(head_width)
    rows = HEADS * tokens
    heads = jnp.where(
        jnp.right_shift(iota((rows, width), 0), tokens.bit_length() - 1)
        == jnp.right_shift(iota((rows, width), 1), head_width.bit_length() - 1),
        1.0, 0.0,
    )
    heads_b = heads.astype(BF)

    def spread(values):
        return jnp.concatenate([values] * HEADS, axis=0) * heads_b

    def gather_heads(values):
        return jnp.sum((values * heads).reshape(HEADS, tokens, width), axis=0)

    qx = spread(q)
    logits = mm_nt(k, qx) * scale
    weights = jnp.exp(logits - jnp.max(logits, axis=0, keepdims=True))
    enc_p = weights / jnp.sum(weights, axis=0, keepdims=True)
    enc_pb = enc_p.astype(BF)
    enc_ctx = gather_heads(mm_tn(enc_pb, v)).astype(BF)
    encoded = (tok + mm(enc_ctx, enc_out[...])).astype(BF)
    to_slots(1, by_token, encoded)
    all_to_all_start(1)

    w_mid = win[:, pl.ds(pl.multiple_of(g * tiles, tiles), tiles)]
    w_low = win[:, pl.ds(pl.multiple_of(jnp.maximum(g - 1, 0) * tiles, tiles), tiles)]
    w_high = win[:, pl.ds(pl.multiple_of(jnp.minimum(g + 1, groups - 1) * tiles, tiles), tiles)]
    w_low = jnp.where(g > 0, w_low, -2)
    w_high = jnp.where(g < groups - 1, w_high, -2)
    first_w, last_w = w_mid[:, :1], w_mid[:, tiles - 1 :]
    w_a = jnp.where((w_mid == first_w) | (w_low == first_w), first_w, -1)
    w_b = jnp.where((w_mid == last_w) | (w_high == last_w), last_w, -1)
    mid_columns = as_columns(w_mid)
    in_a = mid_columns[:, :1] == first_w
    in_b = mid_columns[:, :1] == last_w
    vis_low = is_visible(t_col - tiles)
    vis_high = is_visible(t_col + tiles)
    blank = mask_token[...]
    near_columns(enc_ctx, enc_a_send)
    halo_wait(0, og, og_halo)
    dctx_low = mm_nt(og_halo[0], dec_out[...])
    dctx_high = mm_nt(og_halo[1], dec_out[...])
    dctx_a = jnp.where(in_a, dctx_mid.astype(F32), dctx_low).astype(BF)
    dctx_b = jnp.where(in_b, dctx_mid.astype(F32), dctx_high).astype(BF)
    lane = iota((1, 2 * head_width), 1)
    half0 = jnp.where(lane < head_width, 1.0, 0.0).astype(BF)
    half1 = jnp.where(lane < head_width, 0.0, 1.0).astype(BF)
    scaled0, scaled1 = half0 * BF(scale), half1 * BF(scale)
    at_a, at_b = w_mid == first_w, w_mid == last_w

    def same_window(row):
        same = jnp.where(as_columns(row) == row, 0.0, NEG)
        return jnp.concatenate([same, same], axis=1)

    def diagonal(values):
        return jnp.concatenate(
            [values[:head_width, :tiles], values[head_width:, tiles:]], axis=0
        )

    def window_block(qkv, dctx, row, keep_rows, keep_lanes):
        bias = same_window(row)
        for pair in range(HEADS // 2):
            at = slice(pair * 2 * head_width, (pair + 1) * 2 * head_width)
            qs, ks, vs = qkv[0][:, at], qkv[1][:, at], qkv[2][:, at]
            do = dctx[:, at]
            qx = jnp.concatenate([qs * scaled0, qs * scaled1], axis=0)
            dox = jnp.concatenate([do * half0, do * half1], axis=0)
            scores = mm_nt(ks, qx) + bias
            e = jnp.exp(scores - jnp.max(scores, axis=0, keepdims=True))
            p = e * (1.0 / jnp.sum(e, axis=0, keepdims=True))
            pb = p.astype(BF)
            dp = mm_nt(vs, dox)
            dsb = (p * (dp - jnp.sum(p * dp, axis=0, keepdims=True))).astype(BF)
            o = diagonal(mm_tn(vs, pb))
            dq = diagonal(mm_tn(ks, dsb))
            dk = mm(dsb, qx)
            dv = mm(pb, dox)
            at_v = slice(width + at.start, width + at.stop)
            if keep_rows is not None:
                o = jnp.where(keep_lanes, o, acc_o[at])
                dq = jnp.where(keep_lanes, dq, acc_q[at])
                dk = jnp.where(keep_rows, dk, acc_kv[:, at])
                dv = jnp.where(keep_rows, dv, acc_kv[:, at_v])
            acc_o[at] = o
            acc_q[at] = dq
            acc_kv[:, at] = dk
            acc_kv[:, at_v] = dv

    def dec_project(values, shown):
        x = jnp.where(shown > 0.5, values.astype(F32), blank)
        r = norm_scale(x)
        out = mm((x * r).astype(BF), dec_qkv[...])
        return x, r, out

    def split3(values):
        values = values.astype(BF)
        return values[:, :width], values[:, width : 2 * width], values[:, 2 * width :]

    slots = all_to_all_wait(1)
    placed = from_slots(by_tile, slots).astype(BF)
    h_send[...] = placed
    halo_start(1, h_send, h_halo)
    x_mid, r_mid, qkv_mid = dec_project(placed, here)
    dec_b_copies = near_start(0, dec_b_send, dec_b, True)
    window_block(split3(qkv_mid), dctx_mid, w_mid, None, None)
    halo_wait(1, h_send, h_halo)
    _, _, qkv_edge = dec_project(
        h_halo[...].reshape(2 * tiles, width), jnp.concatenate([vis_low, vis_high], axis=0)
    )
    qkv_a = jnp.where(in_a, qkv_mid, qkv_edge[:tiles])
    qkv_b = jnp.where(in_b, qkv_mid, qkv_edge[tiles:])
    window_block(split3(qkv_a), dctx_a, w_a, in_a, at_a)
    window_block(split3(qkv_b), dctx_b, w_b, in_b, at_b)

    grad_q = (acc_q[...].T * scale).astype(BF)
    dnormed = mm_nt(grad_q, dec_qkv[:, :width]) + mm_nt(
        acc_kv[...].astype(BF), dec_qkv[:, width:]
    )
    dinputs = norm_back(x_mid, r_mid, dnormed) + grad_out.astype(F32)
    to_slots(2, by_tile, dinputs.astype(BF))
    all_to_all_start(2)

    near_columns(acc_o[...].astype(BF), dec_a_send, mm_tn)
    dec_a_copies = near_start(1, dec_a_send, dec_a, False)
    grad_enc = from_slots(by_token, all_to_all_wait(2))
    grad_enc_b = grad_enc.astype(BF)
    for j in range(slides):
        enc_b_send[j] = grad_enc_b[:, j * cw : (j + 1) * cw]
    enc_copies = near_start(2, enc_a_send, enc_a, False) + near_start(3, enc_b_send, enc_b, True)
    dox = spread(mm_nt(grad_enc_b, enc_out[...]).astype(BF))
    dp = mm_nt(v, dox)
    dsb = (enc_p * (dp - jnp.sum(enc_p * dp, axis=0, keepdims=True)) * scale).astype(BF)
    dq = gather_heads(mm_tn(dsb, k))
    dk = mm(dsb, qx)
    dv = mm(enc_pb, dox)
    dproj = jnp.concatenate([dq, dk, dv], axis=1).astype(BF)
    dn = mm_nt(dproj, enc_qkv[...]).astype(BF).astype(F32)
    dtok = (norm_back(tok, tok_r, dn) + grad_enc).astype(BF)
    to_slots(3, by_token, dtok)
    all_to_all_start(3)

    for copy in dec_a_copies + dec_b_copies:
        copy.wait_recv()
    dec_own, dec_far = far_start(0, near_product(dec_a, dec_b))
    for copy in enc_copies:
        copy.wait_recv()
    enc_own, enc_far = far_start(1, near_product(enc_a, enc_b))
    out_tiles[0] = from_slots(by_tile, all_to_all_wait(3)).astype(BF)
    out_dec[...] = far_end(dec_own, dec_far, 0)
    out_enc[...] = far_end(enc_own, enc_far, 1)
    for copy in pending:
        copy.wait_send()
    halo_end(0, og, og_halo)
    halo_end(1, h_send, h_halo)


def hand_over(a, b, c, a_out, b_out, c_out, sems):
    pairs = ((a, a_out), (b, b_out), (c, c_out))
    copies = [pltpu.make_async_copy(x, y, sems.at[i]) for i, (x, y) in enumerate(pairs)]
    for copy in copies:
        copy.start()
    for copy in copies:
        copy.wait()


def shards(groups, slides, emb, vis, win, og, mask_token, enc_qkv, enc_out, dec_qkv, dec_out):
    _, tiles, width = emb.shape
    tokens = vis.shape[1] // groups
    near = min(4, groups)
    far = groups // near
    rb, cw = width // groups, width // slides
    span = far * rb
    ns = near * slides
    far_type = BF if rb % 16 == 0 else F32
    dma = pltpu.SemaphoreType.DMA
    vmem = pl.BlockSpec(memory_space=pltpu.VMEM)
    results = pl.pallas_call(
        functools.partial(kernel, groups, slides, near),
        out_shape=(
            jax.ShapeDtypeStruct(emb.shape, BF),
            jax.ShapeDtypeStruct((rb, cw), F32),
            jax.ShapeDtypeStruct((rb, cw), F32),
        ),
        in_specs=[pl.BlockSpec(memory_space=pl.ANY)] * 9,
        out_specs=(vmem,) * 3,
        scratch_shapes=[
            pltpu.VMEM((tiles, width), BF),
            pltpu.VMEM(vis.shape, I32),
            pltpu.VMEM(win.shape, I32),
            pltpu.VMEM((tiles, width), BF),
            pltpu.VMEM((1, width), F32),
            pltpu.VMEM(enc_qkv.shape, BF),
            pltpu.VMEM(enc_out.shape, BF),
            pltpu.VMEM(dec_qkv.shape, BF),
            pltpu.VMEM(dec_out.shape, BF),
            pltpu.VMEM((4, groups, 2 * CAP, width // 2), BF),
            pltpu.VMEM((4, groups, 2 * CAP, width // 2), BF),
            pltpu.VMEM((2, tiles, width), BF),
            pltpu.VMEM((tiles, width), BF),
            pltpu.VMEM((2, tiles, width), BF),
            pltpu.VMEM((near, tiles, span), BF),
            pltpu.VMEM((slides, tiles, cw), BF),
            pltpu.VMEM((ns, tiles, span), BF),
            pltpu.VMEM((ns, tiles, cw), BF),
            pltpu.VMEM((near, tokens, span), BF),
            pltpu.VMEM((slides, tokens, cw), BF),
            pltpu.VMEM((ns, tokens, span), BF),
            pltpu.VMEM((ns, tokens, cw), BF),
            pltpu.VMEM((2, far, rb, cw), far_type),
            pltpu.VMEM((2, far, rb, cw), far_type),
            pltpu.VMEM((far, rb, cw), F32),
            pltpu.VMEM((width, tiles), F32),
            pltpu.VMEM((tiles, 2 * width), F32),
            pltpu.VMEM((width, tiles), F32),
            dma((9,)),
            dma((4, groups)), dma((4, groups)),
            dma((2, 2)), dma((2, 2)),
            dma((4, ns)), dma((4, ns)),
            dma((2, far)), dma((2, far)),
        ],
        compiler_params=pltpu.CompilerParams(
            collective_id=0, has_side_effects=True, vmem_limit_bytes=60 * 1024 * 1024
        ),
    )(emb, vis, win, og, mask_token[None, :], enc_qkv, enc_out, dec_qkv, dec_out)
    return pl.pallas_call(
        hand_over,
        out_shape=tuple(jax.ShapeDtypeStruct(r.shape, r.dtype) for r in results),
        in_specs=[pl.BlockSpec(memory_space=pl.ANY)] * 3,
        out_specs=(pl.BlockSpec(memory_space=pltpu.HBM),) * 3,
        scratch_shapes=[dma((3,))],
    )(*results)


def solution(mesh):
    placed = (
        P("slide", "grid", None),
        P("slide", None),
        P("slide", None),
        P("slide", "grid", None),
        P(),
        P(),
        P(),
        P(),
        P(),
    )
    return jax.shard_map(
        functools.partial(shards, mesh.shape["grid"], mesh.shape["slide"]),
        mesh=mesh,
        in_specs=placed,
        out_specs=(P("slide", "grid", None), P("grid", "slide"), P("grid", "slide")),
        check_vma=False,
    )
```

```python
import functools
import math

import jax
import jax.numpy as jnp
from jax import lax
from jax.experimental import pallas as pl
from jax.experimental.pallas import tpu as pltpu
from jax.sharding import PartitionSpec as P

HEADS = 8
EPS = 1e-06
CAP = 8
NEG = -1e30
BF = jnp.bfloat16
F32 = jnp.float32
I32 = jnp.int32
MESH = pl.DeviceIdType.MESH


def mm(a, b):
    return lax.dot_general(a, b, (((1,), (0,)), ((), ())), preferred_element_type=F32)


def mm_nt(a, b):
    return lax.dot_general(a, b, (((1,), (1,)), ((), ())), preferred_element_type=F32)


def mm_tn(a, b):
    return lax.dot_general(a, b, (((0,), (0,)), ((), ())), preferred_element_type=F32)


def iota(shape, dim):
    return lax.broadcasted_iota(I32, shape, dim)


def norm_scale(x):
    return lax.rsqrt(jnp.mean(x * x, axis=-1, keepdims=True) + EPS)


def norm_back(x, r, dn):
    return r * dn - x * (r * r * r * jnp.mean(dn * x, axis=-1, keepdims=True))


def fold(rows):
    half = rows.shape[1] // 2
    return jnp.concatenate([rows[:, :half], rows[:, half:]], axis=0)


def unfold(rows):
    n = rows.shape[0] // 2
    return jnp.concatenate([rows[:n], rows[n:]], axis=1)


def one_hot(peer, place, count):
    left = peer * (2 * CAP) + place
    ids = jnp.concatenate([left, left + jnp.where(peer < 0, 0, CAP)], axis=0)
    return jnp.where(iota((ids.shape[0], 2 * CAP * count), 1) == ids, 1.0, 0.0).astype(BF)


def as_columns(row):
    n = row.shape[1]
    return jnp.broadcast_to(row, (n, n)).T


def kernel(
    groups, slides, near,
    emb_in, vis_in, win_in, og_in, mask_in, enc_qkv_in, enc_out_in, dec_qkv_in, dec_out_in,
    out_tiles, out_enc, out_dec,
    emb, vis, win, og, mask_token, enc_qkv, enc_out, dec_qkv, dec_out,
    sbuf, rbuf, og_halo, h_send, h_halo,
    dec_a_send, dec_b_send, dec_a, dec_b,
    enc_a_send, enc_b_send, enc_a, enc_b,
    far_send, far_recv, far_own, acc_q, acc_kv, acc_o, load_s,
    a2a_ss, a2a_rs, halo_ss, halo_rs, near_ss, near_rs, far_ss, far_rs,
):
    s = lax.axis_index("slide")
    g = lax.axis_index("grid")
    tiles, width = emb.shape
    vis_all = vis.shape[1]
    tokens = vis_all // groups
    far = groups // near
    rb, cw = out_enc.shape
    n = lax.rem(g, near)
    f = lax.div(g, near)
    log_g = groups.bit_length() - 1
    pending = []
    loads = []
    for i, (src, dst) in enumerate((
        (vis_in, vis), (emb_in.at[0], emb), (og_in.at[0], og), (enc_qkv_in, enc_qkv),
        (dec_out_in, dec_out), (win_in, win), (enc_out_in, enc_out), (mask_in, mask_token),
        (dec_qkv_in, dec_qkv),
    )):
        loads.append((dst, pltpu.make_async_copy(src, dst, load_s.at[i])))
        loads[i][1].start()

    def loaded(*refs):
        for dst, copy in loads:
            if any(dst is ref for ref in refs):
                copy.wait()

    barrier = pltpu.get_barrier_semaphore()
    met = 0
    for j in range(1, groups):
        pl.semaphore_signal(
            barrier, inc=1, device_id=(s, lax.rem(g + j, groups)), device_id_type=MESH
        )
        met += 1
    for ds in range(1, slides):
        for dn in range(near):
            peer = (lax.rem(s + ds, slides), f * near + lax.rem(n + dn, near))
            pl.semaphore_signal(barrier, inc=1, device_id=peer, device_id_type=MESH)
            met += 1

    def send(src, dst, ss, rs, peer):
        copy = pltpu.make_async_remote_copy(
            src_ref=src, dst_ref=dst, send_sem=ss, recv_sem=rs,
            device_id=peer, device_id_type=MESH,
        )
        copy.start()

    def take(like, sem):
        pltpu.make_async_copy(like, like, sem).wait()

    def all_to_all_start(stage):
        for j in sorted(range(1, groups), key=lambda j: -min(j, groups - j)):
            dst = lax.rem(g + j, groups)
            send(sbuf.at[stage, dst], rbuf.at[stage, g], a2a_ss.at[stage], a2a_rs.at[stage],
                 (s, dst))
        rbuf[stage, g] = sbuf[stage, g]
        pending.append((sbuf.at[stage, pl.ds(0, groups - 1)], a2a_ss.at[stage]))

    def all_to_all_wait(stage):
        take(rbuf.at[stage, pl.ds(0, groups - 1)], a2a_rs.at[stage])
        return rbuf[stage].reshape(groups * 2 * CAP, width // 2)

    def halo_copies(kind, src, dst):
        left = jnp.maximum(g - 1, 0)
        right = jnp.minimum(g + 1, groups - 1)

        def to(side, peer):
            return pltpu.make_async_remote_copy(
                src_ref=src, dst_ref=dst.at[side], send_sem=halo_ss.at[kind, side],
                recv_sem=halo_rs.at[kind, side], device_id=(s, peer), device_id_type=MESH,
            )

        return to(1, left), to(0, right)

    def halo_start(kind, src, dst):
        to_left, to_right = halo_copies(kind, src, dst)

        @pl.when(g > 0)
        def _():
            to_left.start()

        @pl.when(g < groups - 1)
        def _():
            to_right.start()

    def halo_wait(kind, src, dst):
        to_left, to_right = halo_copies(kind, src, dst)

        @pl.when(g > 0)
        def _():
            to_right.wait_recv()

        @pl.when(g == 0)
        def _():
            dst[0] = jnp.zeros(dst.shape[1:], dst.dtype)

        @pl.when(g < groups - 1)
        def _():
            to_left.wait_recv()

        @pl.when(g == groups - 1)
        def _():
            dst[1] = jnp.zeros(dst.shape[1:], dst.dtype)

    def halo_end(kind, src, dst):
        to_left, to_right = halo_copies(kind, src, dst)

        @pl.when(g > 0)
        def _():
            to_left.wait_send()

        @pl.when(g < groups - 1)
        def _():
            to_right.wait_send()

    def near_start(kind, src, dst, by_slide):
        for ds in range(slides):
            for dn in range(near):
                o = ds * near + dn
                s2, n2 = lax.rem(s + ds, slides), lax.rem(n + dn, near)
                part = src.at[s2] if by_slide else src.at[n2]
                if o == 0:
                    dst[0] = part[...]
                else:
                    send(part, dst.at[o], near_ss.at[kind], near_rs.at[kind],
                         (s2, f * near + n2))
        pending.append((dst.at[pl.ds(1, slides * near - 1)], near_ss.at[kind]))

    def near_wait(kind, dst):
        take(dst.at[pl.ds(1, slides * near - 1)], near_rs.at[kind])

    def far_start(which, part):
        cube = part.reshape(far, rb, cw)
        far_own[...] = cube
        far_send[which] = cube.astype(far_send.dtype)
        for df in range(1, far):
            f2 = lax.rem(f + df, far)
            send(far_send.at[which, f2], far_recv.at[which, df], far_ss.at[which],
                 far_rs.at[which], (s, f2 * near + n))
        if far > 1:
            pending.append((far_send.at[which, pl.ds(1, far - 1)], far_ss.at[which]))
        return far_own[f]

    def far_end(own, which):
        if far > 1:
            take(far_recv.at[which, pl.ds(1, far - 1)], far_rs.at[which])
        total = own
        for df in range(1, far):
            total = total + far_recv[which, df].astype(F32)
        return total

    def near_product(a, b):
        return mm_tn(a[...].reshape(-1, a.shape[2]), b[...].reshape(-1, b.shape[2]))

    loaded(vis)
    vis_row = vis[...]
    t_col = g * tiles + iota((tiles, 1), 0)

    def is_visible(ids):
        return jnp.sum(jnp.where(vis_row == ids, 1.0, 0.0), axis=1, keepdims=True)

    rank = jnp.sum(jnp.where(vis_row < t_col, 1.0, 0.0), axis=1, keepdims=True).astype(I32)
    here = is_visible(t_col)
    peer = jnp.where(here > 0.5, jnp.bitwise_and(rank, groups - 1), -1)
    place = jnp.bitwise_and(jnp.right_shift(rank, log_g), CAP - 1)
    by_tile = one_hot(peer, place, groups)

    def to_slots(stage, by_row, rows):
        moved = mm_tn(by_row, fold(rows)).astype(BF)
        sbuf[stage] = moved.reshape(groups, 2 * CAP, width // 2)

    def from_slots(by_row, slots):
        return unfold(mm(by_row, slots))

    loaded(emb)
    to_slots(0, by_tile, emb[...])

    pl.semaphore_wait(barrier, met)
    all_to_all_start(0)
    loaded(og)
    halo_start(0, og, og_halo)

    rank_row = iota((tokens, vis_all), 1)
    mine = rank_row == iota((tokens, vis_all), 0) * groups + g
    token_tile = jnp.sum(
        jnp.where(mine, vis_row.astype(F32), 0.0), axis=1, keepdims=True
    ).astype(I32)
    source = jnp.right_shift(token_tile, tiles.bit_length() - 1)
    by_token = one_hot(source, jnp.bitwise_and(iota((tokens, 1), 0), CAP - 1), groups)
    grad_out = og[...]
    for k in range(slides):
        dec_b_send[k] = grad_out[:, k * cw : (k + 1) * cw]
    loaded(dec_out)
    dctx_mid = mm_nt(grad_out, dec_out[...]).astype(BF)
    new = iota((1, width), 1)
    span = far * rb
    low = jnp.bitwise_and(new, span - 1)
    old = (
        jnp.right_shift(low, rb.bit_length() - 1) * near
        + jnp.right_shift(new, span.bit_length() - 1)
    ) * rb + jnp.bitwise_and(low, rb - 1)
    shuffle = jnp.where(iota((width, width), 0) == old, 1.0, 0.0).astype(BF)

    def near_columns(values, dst, product=mm):
        moved = product(values, shuffle).astype(BF)
        for k in range(near):
            dst[k] = moved[:, k * span : (k + 1) * span]

    loaded(enc_qkv, enc_out, win, mask_token, dec_qkv)
    slots = all_to_all_wait(0)

    tok = from_slots(by_token, slots)
    tok_r = norm_scale(tok)
    proj = mm((tok * tok_r).astype(BF), enc_qkv[...]).astype(BF)
    q, k, v = proj[:, :width], proj[:, width : 2 * width], proj[:, 2 * width :]
    head_width = width // HEADS
    scale = 1.0 / math.sqrt(head_width)
    rows = HEADS * tokens
    heads = jnp.where(
        jnp.right_shift(iota((rows, width), 0), tokens.bit_length() - 1)
        == jnp.right_shift(iota((rows, width), 1), head_width.bit_length() - 1),
        1.0, 0.0,
    )
    heads_b = heads.astype(BF)

    def spread(values):
        return jnp.concatenate([values] * HEADS, axis=0) * heads_b

    def gather_heads(values):
        return jnp.sum((values * heads).reshape(HEADS, tokens, width), axis=0)

    qx = spread(q)
    logits = mm_nt(k, qx) * scale
    weights = jnp.exp(logits - jnp.max(logits, axis=0, keepdims=True))
    enc_p = weights / jnp.sum(weights, axis=0, keepdims=True)
    enc_pb = enc_p.astype(BF)
    enc_ctx = gather_heads(mm_tn(enc_pb, v)).astype(BF)
    encoded = (tok + mm(enc_ctx, enc_out[...])).astype(BF)
    to_slots(1, by_token, encoded)
    all_to_all_start(1)

    w_mid = win[:, pl.ds(pl.multiple_of(g * tiles, tiles), tiles)]
    w_low = win[:, pl.ds(pl.multiple_of(jnp.maximum(g - 1, 0) * tiles, tiles), tiles)]
    w_high = win[:, pl.ds(pl.multiple_of(jnp.minimum(g + 1, groups - 1) * tiles, tiles), tiles)]
    w_low = jnp.where(g > 0, w_low, -2)
    w_high = jnp.where(g < groups - 1, w_high, -2)
    first_w, last_w = w_mid[:, :1], w_mid[:, tiles - 1 :]
    w_a = jnp.where((w_mid == first_w) | (w_low == first_w), first_w, -1)
    w_b = jnp.where((w_mid == last_w) | (w_high == last_w), last_w, -1)
    mid_columns = as_columns(w_mid)
    in_a = mid_columns[:, :1] == first_w
    in_b = mid_columns[:, :1] == last_w
    vis_low = is_visible(t_col - tiles)
    vis_high = is_visible(t_col + tiles)
    blank = mask_token[...]
    near_columns(enc_ctx, enc_a_send)
    halo_wait(0, og, og_halo)
    dctx_low = mm_nt(og_halo[0], dec_out[...])
    dctx_high = mm_nt(og_halo[1], dec_out[...])
    dctx_a = jnp.where(in_a, dctx_mid.astype(F32), dctx_low).astype(BF)
    dctx_b = jnp.where(in_b, dctx_mid.astype(F32), dctx_high).astype(BF)
    lane = iota((1, 2 * head_width), 1)
    half0 = jnp.where(lane < head_width, 1.0, 0.0).astype(BF)
    half1 = jnp.where(lane < head_width, 0.0, 1.0).astype(BF)
    scaled0, scaled1 = half0 * BF(scale), half1 * BF(scale)
    at_a, at_b = w_mid == first_w, w_mid == last_w

    def same_window(row):
        same = jnp.where(as_columns(row) == row, 0.0, NEG)
        return jnp.concatenate([same, same], axis=1)

    def diagonal(values):
        return jnp.concatenate(
            [values[:head_width, :tiles], values[head_width:, tiles:]], axis=0
        )

    def window_block(qkv, dctx, row, keep_rows, keep_lanes):
        bias = same_window(row)
        for pair in range(HEADS // 2):
            at = slice(pair * 2 * head_width, (pair + 1) * 2 * head_width)
            qs, ks, vs = qkv[0][:, at], qkv[1][:, at], qkv[2][:, at]
            do = dctx[:, at]
            qx = jnp.concatenate([qs * scaled0, qs * scaled1], axis=0)
            dox = jnp.concatenate([do * half0, do * half1], axis=0)
            scores = mm_nt(ks, qx) + bias
            e = jnp.exp(scores - jnp.max(scores, axis=0, keepdims=True))
            p = e * (1.0 / jnp.sum(e, axis=0, keepdims=True))
            pb = p.astype(BF)
            dp = mm_nt(vs, dox)
            dsb = (p * (dp - jnp.sum(p * dp, axis=0, keepdims=True))).astype(BF)
            o = diagonal(mm_tn(vs, pb))
            dq = diagonal(mm_tn(ks, dsb))
            dk = mm(dsb, qx)
            dv = mm(pb, dox)
            at_v = slice(width + at.start, width + at.stop)
            if keep_rows is not None:
                o = jnp.where(keep_lanes, o, acc_o[at])
                dq = jnp.where(keep_lanes, dq, acc_q[at])
                dk = jnp.where(keep_rows, dk, acc_kv[:, at])
                dv = jnp.where(keep_rows, dv, acc_kv[:, at_v])
            acc_o[at] = o
            acc_q[at] = dq
            acc_kv[:, at] = dk
            acc_kv[:, at_v] = dv

    def dec_project(values, shown):
        x = jnp.where(shown > 0.5, values.astype(F32), blank)
        r = norm_scale(x)
        out = mm((x * r).astype(BF), dec_qkv[...])
        return x, r, out

    def split3(values):
        values = values.astype(BF)
        return values[:, :width], values[:, width : 2 * width], values[:, 2 * width :]

    slots = all_to_all_wait(1)
    placed = from_slots(by_tile, slots).astype(BF)
    h_send[...] = placed
    halo_start(1, h_send, h_halo)
    x_mid, r_mid, qkv_mid = dec_project(placed, here)
    near_start(0, dec_b_send, dec_b, True)
    window_block(split3(qkv_mid), dctx_mid, w_mid, None, None)
    halo_wait(1, h_send, h_halo)
    _, _, qkv_edge = dec_project(
        h_halo[...].reshape(2 * tiles, width), jnp.concatenate([vis_low, vis_high], axis=0)
    )
    qkv_a = jnp.where(in_a, qkv_mid, qkv_edge[:tiles])
    qkv_b = jnp.where(in_b, qkv_mid, qkv_edge[tiles:])
    window_block(split3(qkv_a), dctx_a, w_a, in_a, at_a)
    window_block(split3(qkv_b), dctx_b, w_b, in_b, at_b)

    grad_q = (acc_q[...].T * scale).astype(BF)
    dnormed = mm_nt(grad_q, dec_qkv[:, :width]) + mm_nt(
        acc_kv[...].astype(BF), dec_qkv[:, width:]
    )
    dinputs = norm_back(x_mid, r_mid, dnormed) + grad_out.astype(F32)
    to_slots(2, by_tile, dinputs.astype(BF))
    all_to_all_start(2)

    near_columns(acc_o[...].astype(BF), dec_a_send, mm_tn)
    near_start(1, dec_a_send, dec_a, False)
    grad_enc = from_slots(by_token, all_to_all_wait(2))
    grad_enc_b = grad_enc.astype(BF)
    for j in range(slides):
        enc_b_send[j] = grad_enc_b[:, j * cw : (j + 1) * cw]
    near_start(2, enc_a_send, enc_a, False)
    near_start(3, enc_b_send, enc_b, True)
    dox = spread(mm_nt(grad_enc_b, enc_out[...]).astype(BF))
    dp = mm_nt(v, dox)
    dsb = (enc_p * (dp - jnp.sum(enc_p * dp, axis=0, keepdims=True)) * scale).astype(BF)
    dq = gather_heads(mm_tn(dsb, k))
    dk = mm(dsb, qx)
    dv = mm(enc_pb, dox)
    dproj = jnp.concatenate([dq, dk, dv], axis=1).astype(BF)
    dn = mm_nt(dproj, enc_qkv[...]).astype(BF).astype(F32)
    dtok = (norm_back(tok, tok_r, dn) + grad_enc).astype(BF)
    to_slots(3, by_token, dtok)
    all_to_all_start(3)

    near_wait(0, dec_b)
    near_wait(1, dec_a)
    dec_own = far_start(0, near_product(dec_a, dec_b))
    near_wait(2, enc_a)
    near_wait(3, enc_b)
    enc_own = far_start(1, near_product(enc_a, enc_b))
    out_tiles[0] = from_slots(by_tile, all_to_all_wait(3)).astype(BF)
    out_dec[...] = far_end(dec_own, 0)
    out_enc[...] = far_end(enc_own, 1)
    for like, sem in pending:
        take(like, sem)
    halo_end(0, og, og_halo)
    halo_end(1, h_send, h_halo)


def shards(groups, slides, emb, vis, win, og, mask_token, enc_qkv, enc_out, dec_qkv, dec_out):
    _, tiles, width = emb.shape
    tokens = vis.shape[1] // groups
    near = min(4, groups)
    far = groups // near
    rb, cw = width // groups, width // slides
    span = far * rb
    ns = near * slides
    far_type = BF if rb % 16 == 0 else F32
    dma = pltpu.SemaphoreType.DMA
    operands = [
        pltpu.with_memory_space_constraint(x, pltpu.HBM)
        for x in (emb, vis, win, og, mask_token[None, :], enc_qkv, enc_out, dec_qkv, dec_out)
    ]
    vmem = pl.BlockSpec(memory_space=pltpu.VMEM)
    return pl.pallas_call(
        functools.partial(kernel, groups, slides, near),
        out_shape=(
            jax.ShapeDtypeStruct(emb.shape, BF),
            jax.ShapeDtypeStruct((rb, cw), F32),
            jax.ShapeDtypeStruct((rb, cw), F32),
        ),
        in_specs=[pl.BlockSpec(memory_space=pl.ANY)] * 9,
        out_specs=(vmem,) * 3,
        scratch_shapes=[
            pltpu.VMEM((tiles, width), BF),
            pltpu.VMEM(vis.shape, I32),
            pltpu.VMEM(win.shape, I32),
            pltpu.VMEM((tiles, width), BF),
            pltpu.VMEM((1, width), F32),
            pltpu.VMEM(enc_qkv.shape, BF),
            pltpu.VMEM(enc_out.shape, BF),
            pltpu.VMEM(dec_qkv.shape, BF),
            pltpu.VMEM(dec_out.shape, BF),
            pltpu.VMEM((4, groups, 2 * CAP, width // 2), BF),
            pltpu.VMEM((4, groups, 2 * CAP, width // 2), BF),
            pltpu.VMEM((2, tiles, width), BF),
            pltpu.VMEM((tiles, width), BF),
            pltpu.VMEM((2, tiles, width), BF),
            pltpu.VMEM((near, tiles, span), BF),
            pltpu.VMEM((slides, tiles, cw), BF),
            pltpu.VMEM((ns, tiles, span), BF),
            pltpu.VMEM((ns, tiles, cw), BF),
            pltpu.VMEM((near, tokens, span), BF),
            pltpu.VMEM((slides, tokens, cw), BF),
            pltpu.VMEM((ns, tokens, span), BF),
            pltpu.VMEM((ns, tokens, cw), BF),
            pltpu.VMEM((2, far, rb, cw), far_type),
            pltpu.VMEM((2, far, rb, cw), far_type),
            pltpu.VMEM((far, rb, cw), F32),
            pltpu.VMEM((width, tiles), F32),
            pltpu.VMEM((tiles, 2 * width), F32),
            pltpu.VMEM((width, tiles), F32),
            dma((9,)),
            dma((4,)), dma((4,)),
            dma((2, 2)), dma((2, 2)),
            dma((4,)), dma((4,)),
            dma((2,)), dma((2,)),
        ],
        compiler_params=pltpu.CompilerParams(
            collective_id=0, has_side_effects=True, vmem_limit_bytes=44 * 1024 * 1024
        ),
    )(*operands)


def solution(mesh):
    placed = (
        P("slide", "grid", None),
        P("slide", None),
        P("slide", None),
        P("slide", "grid", None),
        P(),
        P(),
        P(),
        P(),
        P(),
    )
    return jax.shard_map(
        functools.partial(shards, mesh.shape["grid"], mesh.shape["slide"]),
        mesh=mesh,
        in_specs=placed,
        out_specs=(P("slide", "grid", None), P("grid", "slide"), P("grid", "slide")),
        check_vma=False,
    )
```

```python
import functools
import math

import jax
import jax.numpy as jnp
from jax import lax
from jax.experimental import pallas as pl
from jax.experimental.pallas import tpu as pltpu
from jax.sharding import PartitionSpec as P

HEADS = 8
EPS = 1e-06
CAP = 8
NEG = -1e30
BF = jnp.bfloat16
F32 = jnp.float32
I32 = jnp.int32
MESH = pl.DeviceIdType.MESH


def mm(a, b):
    return lax.dot_general(a, b, (((1,), (0,)), ((), ())), preferred_element_type=F32)


def mm_nt(a, b):
    return lax.dot_general(a, b, (((1,), (1,)), ((), ())), preferred_element_type=F32)


def mm_tn(a, b):
    return lax.dot_general(a, b, (((0,), (0,)), ((), ())), preferred_element_type=F32)


def iota(shape, dim):
    return lax.broadcasted_iota(I32, shape, dim)


def norm_scale(x):
    return lax.rsqrt(jnp.mean(x * x, axis=-1, keepdims=True) + EPS)


def norm_back(x, r, dn):
    return r * dn - x * (r * r * r * jnp.mean(dn * x, axis=-1, keepdims=True))


def fold(rows):
    half = rows.shape[1] // 2
    return jnp.concatenate([rows[:, :half], rows[:, half:]], axis=0)


def unfold(rows):
    n = rows.shape[0] // 2
    return jnp.concatenate([rows[:n], rows[n:]], axis=1)


def one_hot(peer, place, count):
    left = peer * (2 * CAP) + place
    ids = jnp.concatenate([left, left + jnp.where(peer < 0, 0, CAP)], axis=0)
    return jnp.where(iota((ids.shape[0], 2 * CAP * count), 1) == ids, 1.0, 0.0).astype(BF)


def as_columns(row):
    n = row.shape[1]
    return jnp.broadcast_to(row, (n, n)).T


def kernel(
    groups, slides, near,
    emb_in, vis_in, win_in, og_in, mask_in, enc_qkv_in, enc_out_in, dec_qkv_in, dec_out_in,
    out_tiles, out_enc, out_dec,
    emb, vis, win, og, mask_token, enc_qkv, enc_out, dec_qkv, dec_out,
    sbuf, rbuf, og_halo, h_send, h_halo,
    dec_a_send, dec_b_send, dec_a, dec_b,
    enc_a_send, enc_b_send, enc_a, enc_b,
    far_send, far_recv, far_own, acc_q, acc_kv, acc_o, load_s,
    a2a_ss, a2a_rs, halo_ss, halo_rs, near_ss, near_rs, far_ss, far_rs,
):
    s = lax.axis_index("slide")
    g = lax.axis_index("grid")
    tiles, width = emb.shape
    vis_all = vis.shape[1]
    tokens = vis_all // groups
    far = groups // near
    rb, cw = out_enc.shape
    n = lax.rem(g, near)
    f = lax.div(g, near)
    log_g = groups.bit_length() - 1
    pending = []
    loads = []
    for i, (src, dst) in enumerate((
        (vis_in, vis), (emb_in.at[0], emb), (og_in.at[0], og), (enc_qkv_in, enc_qkv),
        (dec_out_in, dec_out), (win_in, win), (enc_out_in, enc_out), (mask_in, mask_token),
        (dec_qkv_in, dec_qkv),
    )):
        loads.append((dst, pltpu.make_async_copy(src, dst, load_s.at[i])))
    for _, copy in loads[:3]:
        copy.start()

    def wrap(index, count):
        return index - count * jnp.minimum(jnp.maximum(index - (count - 1), 0), 1)

    def loaded(*refs):
        for dst, copy in loads:
            if any(dst is ref for ref in refs):
                copy.wait()

    barrier = pltpu.get_barrier_semaphore()
    met = 0
    for j in range(1, groups):
        pl.semaphore_signal(
            barrier, inc=1, device_id=(s, wrap(g + j, groups)), device_id_type=MESH
        )
        met += 1
    for ds in range(1, slides):
        for dn in range(near):
            peer = (wrap(s + ds, slides), f * near + wrap(n + dn, near))
            pl.semaphore_signal(barrier, inc=1, device_id=peer, device_id_type=MESH)
            met += 1

    def send(src, dst, ss, rs, peer):
        copy = pltpu.make_async_remote_copy(
            src_ref=src, dst_ref=dst, send_sem=ss, recv_sem=rs,
            device_id=peer, device_id_type=MESH,
        )
        copy.start()

    def take(like, sem):
        pltpu.make_async_copy(like, like, sem).wait()

    def all_to_all_start(stage):
        for j in sorted(range(1, groups), key=lambda j: -min(j, groups - j)):
            dst = wrap(g + j, groups)
            send(sbuf.at[stage, dst], rbuf.at[stage, g], a2a_ss.at[stage], a2a_rs.at[stage],
                 (s, dst))
        rbuf[stage, g] = sbuf[stage, g]
        pending.append((sbuf.at[stage, pl.ds(0, groups - 1)], a2a_ss.at[stage]))

    def all_to_all_wait(stage):
        take(rbuf.at[stage, pl.ds(0, groups - 1)], a2a_rs.at[stage])
        return rbuf[stage].reshape(groups * 2 * CAP, width // 2)

    def halo_copies(kind, src, dst):
        left = jnp.maximum(g - 1, 0)
        right = jnp.minimum(g + 1, groups - 1)

        def to(side, peer):
            return pltpu.make_async_remote_copy(
                src_ref=src, dst_ref=dst.at[side], send_sem=halo_ss.at[kind, side],
                recv_sem=halo_rs.at[kind, side], device_id=(s, peer), device_id_type=MESH,
            )

        return to(1, left), to(0, right)

    def halo_start(kind, src, dst):
        to_left, to_right = halo_copies(kind, src, dst)

        @pl.when(g > 0)
        def _():
            to_left.start()

        @pl.when(g < groups - 1)
        def _():
            to_right.start()

    def halo_wait(kind, src, dst):
        to_left, to_right = halo_copies(kind, src, dst)

        @pl.when(g > 0)
        def _():
            to_right.wait_recv()

        @pl.when(g == 0)
        def _():
            dst[0] = jnp.zeros(dst.shape[1:], dst.dtype)

        @pl.when(g < groups - 1)
        def _():
            to_left.wait_recv()

        @pl.when(g == groups - 1)
        def _():
            dst[1] = jnp.zeros(dst.shape[1:], dst.dtype)

    def halo_end(kind, src, dst):
        to_left, to_right = halo_copies(kind, src, dst)

        @pl.when(g > 0)
        def _():
            to_left.wait_send()

        @pl.when(g < groups - 1)
        def _():
            to_right.wait_send()

    def near_start(kind, src, dst, by_slide):
        for ds in range(slides):
            for dn in range(near):
                o = ds * near + dn
                s2, n2 = wrap(s + ds, slides), wrap(n + dn, near)
                part = src.at[s2] if by_slide else src.at[n2]
                if o == 0:
                    dst[0] = part[...]
                else:
                    send(part, dst.at[o], near_ss.at[kind], near_rs.at[kind],
                         (s2, f * near + n2))
        pending.append((dst.at[pl.ds(1, slides * near - 1)], near_ss.at[kind]))

    def near_wait(kind, dst):
        take(dst.at[pl.ds(1, slides * near - 1)], near_rs.at[kind])

    def far_start(which, part):
        cube = part.reshape(far, rb, cw)
        far_own[...] = cube
        far_send[which] = cube.astype(far_send.dtype)
        for df in range(1, far):
            f2 = wrap(f + df, far)
            send(far_send.at[which, f2], far_recv.at[which, df], far_ss.at[which],
                 far_rs.at[which], (s, f2 * near + n))
        if far > 1:
            pending.append((far_send.at[which, pl.ds(1, far - 1)], far_ss.at[which]))
        return far_own[f]

    def far_end(own, which):
        if far > 1:
            take(far_recv.at[which, pl.ds(1, far - 1)], far_rs.at[which])
        total = own
        for df in range(1, far):
            total = total + far_recv[which, df].astype(F32)
        return total

    def near_product(a, b):
        return mm_tn(a[...].reshape(-1, a.shape[2]), b[...].reshape(-1, b.shape[2]))

    loaded(vis)
    vis_row = vis[...]
    t_col = g * tiles + iota((tiles, 1), 0)

    def is_visible(ids):
        return jnp.sum(jnp.where(vis_row == ids, 1.0, 0.0), axis=1, keepdims=True)

    rank = jnp.sum(jnp.where(vis_row < t_col, 1.0, 0.0), axis=1, keepdims=True).astype(I32)
    here = is_visible(t_col)
    peer = jnp.where(here > 0.5, jnp.bitwise_and(rank, groups - 1), -1)
    place = jnp.bitwise_and(jnp.right_shift(rank, log_g), CAP - 1)
    by_tile = one_hot(peer, place, groups)

    def to_slots(stage, by_row, rows):
        moved = mm_tn(by_row, fold(rows)).astype(BF)
        sbuf[stage] = moved.reshape(groups, 2 * CAP, width // 2)

    def from_slots(by_row, slots):
        return unfold(mm(by_row, slots))

    loaded(emb)
    for _, copy in loads[3:]:
        copy.start()
    to_slots(0, by_tile, emb[...])

    pl.semaphore_wait(barrier, met)
    all_to_all_start(0)
    loaded(og)
    halo_start(0, og, og_halo)

    rank_row = iota((tokens, vis_all), 1)
    mine = rank_row == iota((tokens, vis_all), 0) * groups + g
    token_tile = jnp.sum(
        jnp.where(mine, vis_row.astype(F32), 0.0), axis=1, keepdims=True
    ).astype(I32)
    source = jnp.right_shift(token_tile, tiles.bit_length() - 1)
    by_token = one_hot(source, jnp.bitwise_and(iota((tokens, 1), 0), CAP - 1), groups)
    grad_out = og[...]
    for k in range(slides):
        dec_b_send[k] = grad_out[:, k * cw : (k + 1) * cw]
    loaded(dec_out)
    dctx_mid = mm_nt(grad_out, dec_out[...]).astype(BF)
    new = iota((1, width), 1)
    span = far * rb
    low = jnp.bitwise_and(new, span - 1)
    old = (
        jnp.right_shift(low, rb.bit_length() - 1) * near
        + jnp.right_shift(new, span.bit_length() - 1)
    ) * rb + jnp.bitwise_and(low, rb - 1)
    shuffle = jnp.where(iota((width, width), 0) == old, 1.0, 0.0).astype(BF)

    def near_columns(values, dst, product=mm):
        moved = product(values, shuffle).astype(BF)
        for k in range(near):
            dst[k] = moved[:, k * span : (k + 1) * span]

    head_width = width // HEADS
    scale = 1.0 / math.sqrt(head_width)
    rows = HEADS * tokens
    heads = jnp.where(
        jnp.right_shift(iota((rows, width), 0), tokens.bit_length() - 1)
        == jnp.right_shift(iota((rows, width), 1), head_width.bit_length() - 1),
        1.0, 0.0,
    )
    heads_b = heads.astype(BF)

    loaded(enc_qkv, enc_out, win, mask_token, dec_qkv)
    slots = all_to_all_wait(0)

    tok = from_slots(by_token, slots)
    tok_r = norm_scale(tok)
    proj = mm((tok * tok_r).astype(BF), enc_qkv[...]).astype(BF)
    q, k, v = proj[:, :width], proj[:, width : 2 * width], proj[:, 2 * width :]
    def spread(values):
        return jnp.concatenate([values] * HEADS, axis=0) * heads_b

    def gather_heads(values):
        return jnp.sum((values * heads).reshape(HEADS, tokens, width), axis=0)

    qx = spread(q)
    logits = mm_nt(k, qx) * scale
    weights = jnp.exp(logits - jnp.max(logits, axis=0, keepdims=True))
    enc_p = weights / jnp.sum(weights, axis=0, keepdims=True)
    enc_pb = enc_p.astype(BF)
    enc_ctx = gather_heads(mm_tn(enc_pb, v)).astype(BF)
    encoded = (tok + mm(enc_ctx, enc_out[...])).astype(BF)
    to_slots(1, by_token, encoded)
    all_to_all_start(1)

    w_mid = win[:, pl.ds(pl.multiple_of(g * tiles, tiles), tiles)]
    w_low = win[:, pl.ds(pl.multiple_of(jnp.maximum(g - 1, 0) * tiles, tiles), tiles)]
    w_high = win[:, pl.ds(pl.multiple_of(jnp.minimum(g + 1, groups - 1) * tiles, tiles), tiles)]
    w_low = jnp.where(g > 0, w_low, -2)
    w_high = jnp.where(g < groups - 1, w_high, -2)
    first_w, last_w = w_mid[:, :1], w_mid[:, tiles - 1 :]
    w_a = jnp.where((w_mid == first_w) | (w_low == first_w), first_w, -1)
    w_b = jnp.where((w_mid == last_w) | (w_high == last_w), last_w, -1)
    mid_columns = as_columns(w_mid)
    in_a = mid_columns[:, :1] == first_w
    in_b = mid_columns[:, :1] == last_w
    vis_low = is_visible(t_col - tiles)
    vis_high = is_visible(t_col + tiles)
    blank = mask_token[...]
    near_columns(enc_ctx, enc_a_send)
    halo_wait(0, og, og_halo)
    dctx_edge = mm_nt(og_halo[...].reshape(2 * tiles, width), dec_out[...])
    dctx_low, dctx_high = dctx_edge[:tiles], dctx_edge[tiles:]
    dctx_a = jnp.where(in_a, dctx_mid.astype(F32), dctx_low).astype(BF)
    dctx_b = jnp.where(in_b, dctx_mid.astype(F32), dctx_high).astype(BF)
    lane = iota((1, 2 * head_width), 1)
    half0 = jnp.where(lane < head_width, 1.0, 0.0).astype(BF)
    half1 = jnp.where(lane < head_width, 0.0, 1.0).astype(BF)
    scaled0, scaled1 = half0 * BF(scale), half1 * BF(scale)
    at_a, at_b = w_mid == first_w, w_mid == last_w

    def same_window(row):
        same = jnp.where(as_columns(row) == row, 0.0, NEG)
        return jnp.concatenate([same, same], axis=1)

    def diagonal(values):
        return jnp.concatenate(
            [values[:head_width, :tiles], values[head_width:, tiles:]], axis=0
        )

    def window_block(qkv, dctx, row, keep_rows, keep_lanes):
        bias = same_window(row)
        for pair in range(HEADS // 2):
            at = slice(pair * 2 * head_width, (pair + 1) * 2 * head_width)
            qs, ks, vs = qkv[0][:, at], qkv[1][:, at], qkv[2][:, at]
            do = dctx[:, at]
            qx = jnp.concatenate([qs * scaled0, qs * scaled1], axis=0)
            dox = jnp.concatenate([do * half0, do * half1], axis=0)
            scores = mm_nt(ks, qx) + bias
            e = jnp.exp(scores - jnp.max(scores, axis=0, keepdims=True))
            p = e * (1.0 / jnp.sum(e, axis=0, keepdims=True))
            pb = p.astype(BF)
            dp = mm_nt(vs, dox)
            dsb = (p * (dp - jnp.sum(p * dp, axis=0, keepdims=True))).astype(BF)
            o = diagonal(mm_tn(vs, pb))
            dq = diagonal(mm_tn(ks, dsb))
            dk = mm(dsb, qx)
            dv = mm(pb, dox)
            at_v = slice(width + at.start, width + at.stop)
            if keep_rows is not None:
                o = jnp.where(keep_lanes, o, acc_o[at])
                dq = jnp.where(keep_lanes, dq, acc_q[at])
                dk = jnp.where(keep_rows, dk, acc_kv[:, at])
                dv = jnp.where(keep_rows, dv, acc_kv[:, at_v])
            acc_o[at] = o
            acc_q[at] = dq
            acc_kv[:, at] = dk
            acc_kv[:, at_v] = dv

    def dec_project(values, shown):
        x = jnp.where(shown > 0.5, values.astype(F32), blank)
        r = norm_scale(x)
        out = mm((x * r).astype(BF), dec_qkv[...])
        return x, r, out

    def split3(values):
        values = values.astype(BF)
        return values[:, :width], values[:, width : 2 * width], values[:, 2 * width :]

    slots = all_to_all_wait(1)
    placed = from_slots(by_tile, slots).astype(BF)
    h_send[...] = placed
    halo_start(1, h_send, h_halo)
    x_mid, r_mid, qkv_mid = dec_project(placed, here)
    window_block(split3(qkv_mid), dctx_mid, w_mid, None, None)
    halo_wait(1, h_send, h_halo)
    near_start(0, dec_b_send, dec_b, True)
    _, _, qkv_edge = dec_project(
        h_halo[...].reshape(2 * tiles, width), jnp.concatenate([vis_low, vis_high], axis=0)
    )
    qkv_a = jnp.where(in_a, qkv_mid, qkv_edge[:tiles])
    qkv_b = jnp.where(in_b, qkv_mid, qkv_edge[tiles:])
    window_block(split3(qkv_a), dctx_a, w_a, in_a, at_a)
    window_block(split3(qkv_b), dctx_b, w_b, in_b, at_b)

    grad_q = (acc_q[...].T * scale).astype(BF)
    dnormed = mm_nt(grad_q, dec_qkv[:, :width]) + mm_nt(
        acc_kv[...].astype(BF), dec_qkv[:, width:]
    )
    dinputs = norm_back(x_mid, r_mid, dnormed) + grad_out.astype(F32)
    to_slots(2, by_tile, dinputs.astype(BF))
    all_to_all_start(2)

    near_columns(acc_o[...].astype(BF), dec_a_send, mm_tn)
    near_start(1, dec_a_send, dec_a, False)
    grad_enc = from_slots(by_token, all_to_all_wait(2))
    grad_enc_b = grad_enc.astype(BF)
    for j in range(slides):
        enc_b_send[j] = grad_enc_b[:, j * cw : (j + 1) * cw]
    near_start(2, enc_a_send, enc_a, False)
    near_start(3, enc_b_send, enc_b, True)
    dox = spread(mm_nt(grad_enc_b, enc_out[...]).astype(BF))
    dp = mm_nt(v, dox)
    dsb = (enc_p * (dp - jnp.sum(enc_p * dp, axis=0, keepdims=True)) * scale).astype(BF)
    dq = gather_heads(mm_tn(dsb, k))
    dk = mm(dsb, qx)
    dv = mm(enc_pb, dox)
    dproj = jnp.concatenate([dq, dk, dv], axis=1).astype(BF)
    dn = mm_nt(dproj, enc_qkv[...]).astype(BF).astype(F32)
    dtok = (norm_back(tok, tok_r, dn) + grad_enc).astype(BF)
    to_slots(3, by_token, dtok)
    all_to_all_start(3)

    near_wait(0, dec_b)
    near_wait(1, dec_a)
    dec_own = far_start(0, near_product(dec_a, dec_b))
    near_wait(2, enc_a)
    near_wait(3, enc_b)
    enc_own = far_start(1, near_product(enc_a, enc_b))
    out_tiles[0] = from_slots(by_tile, all_to_all_wait(3)).astype(BF)
    out_dec[...] = far_end(dec_own, 0)
    out_enc[...] = far_end(enc_own, 1)
    for like, sem in pending:
        take(like, sem)
    halo_end(0, og, og_halo)
    halo_end(1, h_send, h_halo)


def shards(groups, slides, emb, vis, win, og, mask_token, enc_qkv, enc_out, dec_qkv, dec_out):
    _, tiles, width = emb.shape
    tokens = vis.shape[1] // groups
    near = min(4, groups)
    far = groups // near
    rb, cw = width // groups, width // slides
    span = far * rb
    ns = near * slides
    far_type = BF if rb % 16 == 0 else F32
    dma = pltpu.SemaphoreType.DMA
    operands = [
        pltpu.with_memory_space_constraint(x, pltpu.HBM)
        for x in (emb, vis, win, og, mask_token[None, :], enc_qkv, enc_out, dec_qkv, dec_out)
    ]
    vmem = pl.BlockSpec(memory_space=pltpu.VMEM)
    return pl.pallas_call(
        functools.partial(kernel, groups, slides, near),
        out_shape=(
            jax.ShapeDtypeStruct(emb.shape, BF),
            jax.ShapeDtypeStruct((rb, cw), F32),
            jax.ShapeDtypeStruct((rb, cw), F32),
        ),
        in_specs=[pl.BlockSpec(memory_space=pl.ANY)] * 9,
        out_specs=(vmem,) * 3,
        scratch_shapes=[
            pltpu.VMEM((tiles, width), BF),
            pltpu.VMEM(vis.shape, I32),
            pltpu.VMEM(win.shape, I32),
            pltpu.VMEM((tiles, width), BF),
            pltpu.VMEM((1, width), F32),
            pltpu.VMEM(enc_qkv.shape, BF),
            pltpu.VMEM(enc_out.shape, BF),
            pltpu.VMEM(dec_qkv.shape, BF),
            pltpu.VMEM(dec_out.shape, BF),
            pltpu.VMEM((4, groups, 2 * CAP, width // 2), BF),
            pltpu.VMEM((4, groups, 2 * CAP, width // 2), BF),
            pltpu.VMEM((2, tiles, width), BF),
            pltpu.VMEM((tiles, width), BF),
            pltpu.VMEM((2, tiles, width), BF),
            pltpu.VMEM((near, tiles, span), BF),
            pltpu.VMEM((slides, tiles, cw), BF),
            pltpu.VMEM((ns, tiles, span), BF),
            pltpu.VMEM((ns, tiles, cw), BF),
            pltpu.VMEM((near, tokens, span), BF),
            pltpu.VMEM((slides, tokens, cw), BF),
            pltpu.VMEM((ns, tokens, span), BF),
            pltpu.VMEM((ns, tokens, cw), BF),
            pltpu.VMEM((2, far, rb, cw), far_type),
            pltpu.VMEM((2, far, rb, cw), far_type),
            pltpu.VMEM((far, rb, cw), F32),
            pltpu.VMEM((width, tiles), F32),
            pltpu.VMEM((tiles, 2 * width), F32),
            pltpu.VMEM((width, tiles), F32),
            dma((9,)),
            dma((4,)), dma((4,)),
            dma((2, 2)), dma((2, 2)),
            dma((4,)), dma((4,)),
            dma((2,)), dma((2,)),
        ],
        compiler_params=pltpu.CompilerParams(
            collective_id=0, has_side_effects=True, vmem_limit_bytes=44 * 1024 * 1024
        ),
    )(*operands)


def solution(mesh):
    placed = (
        P("slide", "grid", None),
        P("slide", None),
        P("slide", None),
        P("slide", "grid", None),
        P(),
        P(),
        P(),
        P(),
        P(),
    )
    return jax.shard_map(
        functools.partial(shards, mesh.shape["grid"], mesh.shape["slide"]),
        mesh=mesh,
        in_specs=placed,
        out_specs=(P("slide", "grid", None), P("grid", "slide"), P("grid", "slide")),
        check_vma=False,
    )
```

```python
import functools
import math

import jax
import jax.numpy as jnp
from jax import lax
from jax.experimental import pallas as pl
from jax.experimental.pallas import tpu as pltpu
from jax.sharding import PartitionSpec as P

HEADS = 8
EPS = 1e-06
CAP = 8
NEG = -1e30
BF = jnp.bfloat16
F32 = jnp.float32
I32 = jnp.int32
MESH = pl.DeviceIdType.MESH


def mm(a, b):
    return lax.dot_general(a, b, (((1,), (0,)), ((), ())), preferred_element_type=F32)


def mm_nt(a, b):
    return lax.dot_general(a, b, (((1,), (1,)), ((), ())), preferred_element_type=F32)


def mm_tn(a, b):
    return lax.dot_general(a, b, (((0,), (0,)), ((), ())), preferred_element_type=F32)


def iota(shape, dim):
    return lax.broadcasted_iota(I32, shape, dim)


def norm_scale(x):
    return lax.rsqrt(jnp.mean(x * x, axis=-1, keepdims=True) + EPS)


def norm_back(x, r, dn):
    return r * dn - x * (r * r * r * jnp.mean(dn * x, axis=-1, keepdims=True))


def fold(rows):
    half = rows.shape[1] // 2
    return jnp.concatenate([rows[:, :half], rows[:, half:]], axis=0)


def unfold(rows):
    n = rows.shape[0] // 2
    return jnp.concatenate([rows[:n], rows[n:]], axis=1)


def one_hot(peer, place, count):
    left = peer * (2 * CAP) + place
    ids = jnp.concatenate([left, left + jnp.where(peer < 0, 0, CAP)], axis=0)
    return jnp.where(iota((ids.shape[0], 2 * CAP * count), 1) == ids, 1.0, 0.0).astype(BF)


def as_columns(row):
    n = row.shape[1]
    return jnp.broadcast_to(row, (n, n)).T


def kernel(
    groups, slides, near,
    emb_in, vis_in, win_in, og_in, mask_in, enc_qkv_in, enc_out_in, dec_qkv_in, dec_out_in,
    out_tiles, out_enc, out_dec,
    emb, vis, win, og, mask_token, enc_qkv, enc_out, dec_qkv, dec_out,
    sbuf, rbuf, og_halo, h_send, h_halo,
    dec_a_send, dec_b_send, dec_a, dec_b,
    enc_a_send, enc_b_send, enc_a, enc_b,
    far_send, far_recv, far_own, acc_q, acc_kv, probs, load_s,
    a2a_ss, a2a_rs, halo_ss, halo_rs, near_ss, near_rs, far_ss, far_rs,
):
    s = lax.axis_index("slide")
    g = lax.axis_index("grid")
    tiles, width = emb.shape
    vis_all = vis.shape[1]
    tokens = vis_all // groups
    far = groups // near
    rb, cw = out_enc.shape
    n = lax.rem(g, near)
    f = lax.div(g, near)
    log_g = groups.bit_length() - 1
    pending = []
    loads = []
    for i, (src, dst) in enumerate((
        (vis_in, vis), (emb_in.at[0], emb), (og_in.at[0], og), (enc_qkv_in, enc_qkv),
        (dec_out_in, dec_out), (win_in, win), (enc_out_in, enc_out), (mask_in, mask_token),
        (dec_qkv_in, dec_qkv),
    )):
        loads.append((dst, pltpu.make_async_copy(src, dst, load_s.at[i])))
    for _, copy in loads[:3]:
        copy.start()

    def wrap(index, count):
        return index - count * jnp.minimum(jnp.maximum(index - (count - 1), 0), 1)

    def loaded(*refs):
        for dst, copy in loads:
            if any(dst is ref for ref in refs):
                copy.wait()

    barrier = pltpu.get_barrier_semaphore()
    met = 0
    for j in range(1, groups):
        pl.semaphore_signal(
            barrier, inc=1, device_id=(s, wrap(g + j, groups)), device_id_type=MESH
        )
        met += 1
    for ds in range(1, slides):
        for dn in range(near):
            peer = (wrap(s + ds, slides), f * near + wrap(n + dn, near))
            pl.semaphore_signal(barrier, inc=1, device_id=peer, device_id_type=MESH)
            met += 1

    def send(src, dst, ss, rs, peer):
        copy = pltpu.make_async_remote_copy(
            src_ref=src, dst_ref=dst, send_sem=ss, recv_sem=rs,
            device_id=peer, device_id_type=MESH,
        )
        copy.start()

    def take(like, sem):
        pltpu.make_async_copy(like, like, sem).wait()

    def all_to_all_start(stage):
        for j in sorted(range(1, groups), key=lambda j: -min(j, groups - j)):
            dst = wrap(g + j, groups)
            send(sbuf.at[stage, dst], rbuf.at[stage, g], a2a_ss.at[stage], a2a_rs.at[stage],
                 (s, dst))
        rbuf[stage, g] = sbuf[stage, g]
        pending.append((sbuf.at[stage, pl.ds(0, groups - 1)], a2a_ss.at[stage]))

    def all_to_all_wait(stage):
        take(rbuf.at[stage, pl.ds(0, groups - 1)], a2a_rs.at[stage])
        return rbuf[stage].reshape(groups * 2 * CAP, width // 2)

    def halo_copies(kind, src, dst):
        left = jnp.maximum(g - 1, 0)
        right = jnp.minimum(g + 1, groups - 1)

        def to(side, peer):
            return pltpu.make_async_remote_copy(
                src_ref=src, dst_ref=dst.at[side], send_sem=halo_ss.at[kind, side],
                recv_sem=halo_rs.at[kind, side], device_id=(s, peer), device_id_type=MESH,
            )

        return to(1, left), to(0, right)

    def halo_start(kind, src, dst):
        to_left, to_right = halo_copies(kind, src, dst)

        @pl.when(g > 0)
        def _():
            to_left.start()

        @pl.when(g < groups - 1)
        def _():
            to_right.start()

    def halo_wait(kind, src, dst):
        to_left, to_right = halo_copies(kind, src, dst)

        @pl.when(g > 0)
        def _():
            to_right.wait_recv()

        @pl.when(g == 0)
        def _():
            dst[0] = jnp.zeros(dst.shape[1:], dst.dtype)

        @pl.when(g < groups - 1)
        def _():
            to_left.wait_recv()

        @pl.when(g == groups - 1)
        def _():
            dst[1] = jnp.zeros(dst.shape[1:], dst.dtype)

    def halo_end(kind, src, dst):
        to_left, to_right = halo_copies(kind, src, dst)

        @pl.when(g > 0)
        def _():
            to_left.wait_send()

        @pl.when(g < groups - 1)
        def _():
            to_right.wait_send()

    def near_start(kind, src, dst, by_slide):
        for ds in range(slides):
            for dn in range(near):
                o = ds * near + dn
                s2, n2 = wrap(s + ds, slides), wrap(n + dn, near)
                part = src.at[s2] if by_slide else src.at[n2]
                if o == 0:
                    dst[0] = part[...]
                else:
                    send(part, dst.at[o], near_ss.at[kind], near_rs.at[kind],
                         (s2, f * near + n2))
        pending.append((dst.at[pl.ds(1, slides * near - 1)], near_ss.at[kind]))

    def near_wait(kind, dst):
        take(dst.at[pl.ds(1, slides * near - 1)], near_rs.at[kind])

    def far_start(which, part):
        cube = part.reshape(far, rb, cw)
        far_own[...] = cube
        far_send[which] = cube.astype(far_send.dtype)
        for df in range(1, far):
            f2 = wrap(f + df, far)
            send(far_send.at[which, f2], far_recv.at[which, df], far_ss.at[which],
                 far_rs.at[which], (s, f2 * near + n))
        if far > 1:
            pending.append((far_send.at[which, pl.ds(1, far - 1)], far_ss.at[which]))
        return far_own[f]

    def far_end(own, which):
        if far > 1:
            take(far_recv.at[which, pl.ds(1, far - 1)], far_rs.at[which])
        total = own
        for df in range(1, far):
            total = total + far_recv[which, df].astype(F32)
        return total

    def near_product(a, b):
        return mm_tn(a[...].reshape(-1, a.shape[2]), b[...].reshape(-1, b.shape[2]))

    loaded(vis)
    vis_row = vis[...]
    t_col = g * tiles + iota((tiles, 1), 0)

    def is_visible(ids):
        return jnp.sum(jnp.where(vis_row == ids, 1.0, 0.0), axis=1, keepdims=True)

    rank = jnp.sum(jnp.where(vis_row < t_col, 1.0, 0.0), axis=1, keepdims=True).astype(I32)
    here = is_visible(t_col)
    peer = jnp.where(here > 0.5, jnp.bitwise_and(rank, groups - 1), -1)
    place = jnp.bitwise_and(jnp.right_shift(rank, log_g), CAP - 1)
    by_tile = one_hot(peer, place, groups)

    def to_slots(stage, by_row, rows):
        moved = mm_tn(by_row, fold(rows)).astype(BF)
        sbuf[stage] = moved.reshape(groups, 2 * CAP, width // 2)

    def from_slots(by_row, slots):
        return unfold(mm(by_row, slots))

    loaded(emb)
    for _, copy in loads[3:]:
        copy.start()
    to_slots(0, by_tile, emb[...])

    pl.semaphore_wait(barrier, met)
    all_to_all_start(0)
    loaded(og)
    halo_start(0, og, og_halo)

    rank_row = iota((tokens, vis_all), 1)
    mine = rank_row == iota((tokens, vis_all), 0) * groups + g
    token_tile = jnp.sum(
        jnp.where(mine, vis_row.astype(F32), 0.0), axis=1, keepdims=True
    ).astype(I32)
    source = jnp.right_shift(token_tile, tiles.bit_length() - 1)
    by_token = one_hot(source, jnp.bitwise_and(iota((tokens, 1), 0), CAP - 1), groups)
    grad_out = og[...]
    for k in range(slides):
        dec_b_send[k] = grad_out[:, k * cw : (k + 1) * cw]
    loaded(dec_out)
    dctx_mid = mm_nt(grad_out, dec_out[...]).astype(BF)
    new = iota((1, width), 1)
    span = far * rb
    low = jnp.bitwise_and(new, span - 1)
    old = (
        jnp.right_shift(low, rb.bit_length() - 1) * near
        + jnp.right_shift(new, span.bit_length() - 1)
    ) * rb + jnp.bitwise_and(low, rb - 1)
    shuffle = jnp.where(iota((width, width), 0) == old, 1.0, 0.0).astype(BF)

    def near_columns(values, dst, product=mm):
        moved = product(values, shuffle).astype(BF)
        for k in range(near):
            dst[k] = moved[:, k * span : (k + 1) * span]

    head_width = width // HEADS
    scale = 1.0 / math.sqrt(head_width)
    rows = HEADS * tokens
    heads = jnp.where(
        jnp.right_shift(iota((rows, width), 0), tokens.bit_length() - 1)
        == jnp.right_shift(iota((rows, width), 1), head_width.bit_length() - 1),
        1.0, 0.0,
    )
    heads_b = heads.astype(BF)

    loaded(enc_qkv, enc_out, win, mask_token, dec_qkv)
    slots = all_to_all_wait(0)

    tok = from_slots(by_token, slots)
    tok_r = norm_scale(tok)
    proj = mm((tok * tok_r).astype(BF), enc_qkv[...]).astype(BF)
    q, k, v = proj[:, :width], proj[:, width : 2 * width], proj[:, 2 * width :]
    def spread(values):
        return jnp.concatenate([values] * HEADS, axis=0) * heads_b

    def gather_heads(values):
        return jnp.sum((values * heads).reshape(HEADS, tokens, width), axis=0)

    qx = spread(q)
    logits = mm_nt(k, qx) * scale
    weights = jnp.exp(logits - jnp.max(logits, axis=0, keepdims=True))
    enc_p = weights / jnp.sum(weights, axis=0, keepdims=True)
    enc_pb = enc_p.astype(BF)
    enc_ctx = gather_heads(mm_tn(enc_pb, v)).astype(BF)
    encoded = (tok + mm(enc_ctx, enc_out[...])).astype(BF)
    to_slots(1, by_token, encoded)
    all_to_all_start(1)

    w_mid = win[:, pl.ds(pl.multiple_of(g * tiles, tiles), tiles)]
    w_low = win[:, pl.ds(pl.multiple_of(jnp.maximum(g - 1, 0) * tiles, tiles), tiles)]
    w_high = win[:, pl.ds(pl.multiple_of(jnp.minimum(g + 1, groups - 1) * tiles, tiles), tiles)]
    w_low = jnp.where(g > 0, w_low, -2)
    w_high = jnp.where(g < groups - 1, w_high, -2)
    first_w, last_w = w_mid[:, :1], w_mid[:, tiles - 1 :]
    w_a = jnp.where((w_mid == first_w) | (w_low == first_w), first_w, -1)
    w_b = jnp.where((w_mid == last_w) | (w_high == last_w), last_w, -1)
    mid_columns = as_columns(w_mid)
    in_a = mid_columns[:, :1] == first_w
    in_b = mid_columns[:, :1] == last_w
    vis_low = is_visible(t_col - tiles)
    vis_high = is_visible(t_col + tiles)
    blank = mask_token[...]
    near_columns(enc_ctx, enc_a_send)
    halo_wait(0, og, og_halo)
    dctx_edge = mm_nt(og_halo[...].reshape(2 * tiles, width), dec_out[...])
    dctx_low, dctx_high = dctx_edge[:tiles], dctx_edge[tiles:]
    dctx_a = jnp.where(in_a, dctx_mid.astype(F32), dctx_low).astype(BF)
    dctx_b = jnp.where(in_b, dctx_mid.astype(F32), dctx_high).astype(BF)
    lane = iota((1, 2 * head_width), 1)
    half0 = jnp.where(lane < head_width, 1.0, 0.0).astype(BF)
    half1 = jnp.where(lane < head_width, 0.0, 1.0).astype(BF)
    scaled0, scaled1 = half0 * BF(scale), half1 * BF(scale)
    at_a, at_b = w_mid == first_w, w_mid == last_w

    def same_window(row):
        same = jnp.where(as_columns(row) == row, 0.0, NEG)
        return jnp.concatenate([same, same], axis=1)

    def diagonal(values):
        return jnp.concatenate(
            [values[:head_width, :tiles], values[head_width:, tiles:]], axis=0
        )

    def window_block(block, qkv, dctx, row, keep_rows, keep_lanes):
        bias = same_window(row)
        for pair in range(HEADS // 2):
            at = slice(pair * 2 * head_width, (pair + 1) * 2 * head_width)
            qs, ks, vs = qkv[0][:, at], qkv[1][:, at], qkv[2][:, at]
            do = dctx[:, at]
            qx = jnp.concatenate([qs * scaled0, qs * scaled1], axis=0)
            dox = jnp.concatenate([do * half0, do * half1], axis=0)
            scores = mm_nt(ks, qx) + bias
            e = jnp.exp(scores - jnp.max(scores, axis=0, keepdims=True))
            p = e * (1.0 / jnp.sum(e, axis=0, keepdims=True))
            pb = p.astype(BF)
            probs[block, pair] = pb
            dp = mm_nt(vs, dox)
            dsb = (p * (dp - jnp.sum(p * dp, axis=0, keepdims=True))).astype(BF)
            dq = diagonal(mm_tn(ks, dsb))
            dk = mm(dsb, qx)
            dv = mm(pb, dox)
            at_v = slice(width + at.start, width + at.stop)
            if keep_rows is not None:
                dq = jnp.where(keep_lanes, dq, acc_q[at])
                dk = jnp.where(keep_rows, dk, acc_kv[:, at])
                dv = jnp.where(keep_rows, dv, acc_kv[:, at_v])
            acc_q[at] = dq
            acc_kv[:, at] = dk
            acc_kv[:, at_v] = dv

    def window_context(values_of):
        pairs = []
        for pair in range(HEADS // 2):
            at = slice(pair * 2 * head_width, (pair + 1) * 2 * head_width)
            mid, low, high = [
                diagonal(mm_tn(values[:, at], probs[block, pair]))
                for block, values in enumerate(values_of)
            ]
            pairs.append(jnp.where(at_b, high, jnp.where(at_a, low, mid)))
        return jnp.concatenate(pairs, axis=0).astype(BF)

    def dec_project(values, shown):
        x = jnp.where(shown > 0.5, values.astype(F32), blank)
        r = norm_scale(x)
        out = mm((x * r).astype(BF), dec_qkv[...])
        return x, r, out

    def split3(values):
        values = values.astype(BF)
        return values[:, :width], values[:, width : 2 * width], values[:, 2 * width :]

    slots = all_to_all_wait(1)
    placed = from_slots(by_tile, slots).astype(BF)
    h_send[...] = placed
    halo_start(1, h_send, h_halo)
    x_mid, r_mid, qkv_mid = dec_project(placed, here)
    parts_mid = split3(qkv_mid)
    window_block(0, parts_mid, dctx_mid, w_mid, None, None)
    halo_wait(1, h_send, h_halo)
    near_start(0, dec_b_send, dec_b, True)
    _, _, qkv_edge = dec_project(
        h_halo[...].reshape(2 * tiles, width), jnp.concatenate([vis_low, vis_high], axis=0)
    )
    qkv_a = jnp.where(in_a, qkv_mid, qkv_edge[:tiles])
    qkv_b = jnp.where(in_b, qkv_mid, qkv_edge[tiles:])
    parts_a, parts_b = split3(qkv_a), split3(qkv_b)
    window_block(1, parts_a, dctx_a, w_a, in_a, at_a)
    window_block(2, parts_b, dctx_b, w_b, in_b, at_b)

    grad_q = (acc_q[...].T * scale).astype(BF)
    dnormed = mm_nt(grad_q, dec_qkv[:, :width]) + mm_nt(
        acc_kv[...].astype(BF), dec_qkv[:, width:]
    )
    dinputs = norm_back(x_mid, r_mid, dnormed) + grad_out.astype(F32)
    to_slots(2, by_tile, dinputs.astype(BF))
    all_to_all_start(2)

    dec_ctx = window_context((parts_mid[2], parts_a[2], parts_b[2]))
    near_columns(dec_ctx, dec_a_send, mm_tn)
    near_start(1, dec_a_send, dec_a, False)
    grad_enc = from_slots(by_token, all_to_all_wait(2))
    grad_enc_b = grad_enc.astype(BF)
    for j in range(slides):
        enc_b_send[j] = grad_enc_b[:, j * cw : (j + 1) * cw]
    near_start(2, enc_a_send, enc_a, False)
    near_start(3, enc_b_send, enc_b, True)
    dox = spread(mm_nt(grad_enc_b, enc_out[...]).astype(BF))
    dp = mm_nt(v, dox)
    dsb = (enc_p * (dp - jnp.sum(enc_p * dp, axis=0, keepdims=True)) * scale).astype(BF)
    dq = gather_heads(mm_tn(dsb, k))
    dk = mm(dsb, qx)
    dv = mm(enc_pb, dox)
    dproj = jnp.concatenate([dq, dk, dv], axis=1).astype(BF)
    dn = mm_nt(dproj, enc_qkv[...]).astype(BF).astype(F32)
    dtok = (norm_back(tok, tok_r, dn) + grad_enc).astype(BF)
    to_slots(3, by_token, dtok)
    all_to_all_start(3)

    near_wait(0, dec_b)
    near_wait(1, dec_a)
    dec_own = far_start(0, near_product(dec_a, dec_b))
    near_wait(2, enc_a)
    near_wait(3, enc_b)
    enc_own = far_start(1, near_product(enc_a, enc_b))
    out_tiles[0] = from_slots(by_tile, all_to_all_wait(3)).astype(BF)
    out_dec[...] = far_end(dec_own, 0)
    out_enc[...] = far_end(enc_own, 1)
    for like, sem in pending:
        take(like, sem)
    halo_end(0, og, og_halo)
    halo_end(1, h_send, h_halo)


def hand_over(a, b, c, a_out, b_out, c_out, sems):
    pairs = ((a, a_out), (b, b_out), (c, c_out))
    copies = [pltpu.make_async_copy(x, y, sems.at[i]) for i, (x, y) in enumerate(pairs)]
    for copy in copies:
        copy.start()
    for copy in copies:
        copy.wait()


def shards(groups, slides, emb, vis, win, og, mask_token, enc_qkv, enc_out, dec_qkv, dec_out):
    _, tiles, width = emb.shape
    tokens = vis.shape[1] // groups
    near = min(4, groups)
    far = groups // near
    rb, cw = width // groups, width // slides
    span = far * rb
    ns = near * slides
    far_type = BF if rb % 16 == 0 else F32
    dma = pltpu.SemaphoreType.DMA
    operands = [
        pltpu.with_memory_space_constraint(x, pltpu.HBM)
        for x in (emb, vis, win, og, mask_token[None, :], enc_qkv, enc_out, dec_qkv, dec_out)
    ]
    vmem = pl.BlockSpec(memory_space=pltpu.VMEM)
    results = pl.pallas_call(
        functools.partial(kernel, groups, slides, near),
        out_shape=(
            jax.ShapeDtypeStruct(emb.shape, BF),
            jax.ShapeDtypeStruct((rb, cw), F32),
            jax.ShapeDtypeStruct((rb, cw), F32),
        ),
        in_specs=[pl.BlockSpec(memory_space=pl.ANY)] * 9,
        out_specs=(vmem,) * 3,
        scratch_shapes=[
            pltpu.VMEM((tiles, width), BF),
            pltpu.VMEM(vis.shape, I32),
            pltpu.VMEM(win.shape, I32),
            pltpu.VMEM((tiles, width), BF),
            pltpu.VMEM((1, width), F32),
            pltpu.VMEM(enc_qkv.shape, BF),
            pltpu.VMEM(enc_out.shape, BF),
            pltpu.VMEM(dec_qkv.shape, BF),
            pltpu.VMEM(dec_out.shape, BF),
            pltpu.VMEM((4, groups, 2 * CAP, width // 2), BF),
            pltpu.VMEM((4, groups, 2 * CAP, width // 2), BF),
            pltpu.VMEM((2, tiles, width), BF),
            pltpu.VMEM((tiles, width), BF),
            pltpu.VMEM((2, tiles, width), BF),
            pltpu.VMEM((near, tiles, span), BF),
            pltpu.VMEM((slides, tiles, cw), BF),
            pltpu.VMEM((ns, tiles, span), BF),
            pltpu.VMEM((ns, tiles, cw), BF),
            pltpu.VMEM((near, tokens, span), BF),
            pltpu.VMEM((slides, tokens, cw), BF),
            pltpu.VMEM((ns, tokens, span), BF),
            pltpu.VMEM((ns, tokens, cw), BF),
            pltpu.VMEM((2, far, rb, cw), far_type),
            pltpu.VMEM((2, far, rb, cw), far_type),
            pltpu.VMEM((far, rb, cw), F32),
            pltpu.VMEM((width, tiles), F32),
            pltpu.VMEM((tiles, 2 * width), F32),
            pltpu.VMEM((3, HEADS // 2, tiles, 2 * tiles), BF),
            dma((9,)),
            dma((4,)), dma((4,)),
            dma((2, 2)), dma((2, 2)),
            dma((4,)), dma((4,)),
            dma((2,)), dma((2,)),
        ],
        compiler_params=pltpu.CompilerParams(
            collective_id=0, has_side_effects=True, vmem_limit_bytes=44 * 1024 * 1024
        ),
    )(*operands)
    return pl.pallas_call(
        hand_over,
        out_shape=tuple(jax.ShapeDtypeStruct(r.shape, r.dtype) for r in results),
        in_specs=[pl.BlockSpec(memory_space=pltpu.VMEM)] * 3,
        out_specs=(pl.BlockSpec(memory_space=pltpu.HBM),) * 3,
        scratch_shapes=[dma((3,))],
    )(*results)


def solution(mesh):
    placed = (
        P("slide", "grid", None),
        P("slide", None),
        P("slide", None),
        P("slide", "grid", None),
        P(),
        P(),
        P(),
        P(),
        P(),
    )
    return jax.shard_map(
        functools.partial(shards, mesh.shape["grid"], mesh.shape["slide"]),
        mesh=mesh,
        in_specs=placed,
        out_specs=(P("slide", "grid", None), P("grid", "slide"), P("grid", "slide")),
        check_vma=False,
    )
```

```python
import functools
import math

import jax
import jax.numpy as jnp
from jax import lax
from jax.experimental import pallas as pl
from jax.experimental.pallas import tpu as pltpu
from jax.sharding import PartitionSpec as P

HEADS = 8
EPS = 1e-06
CAP = 8
NEG = -1e30
BF = jnp.bfloat16
F32 = jnp.float32
I32 = jnp.int32
MESH = pl.DeviceIdType.MESH


def mm(a, b):
    return lax.dot_general(a, b, (((1,), (0,)), ((), ())), preferred_element_type=F32)


def mm_nt(a, b):
    return lax.dot_general(a, b, (((1,), (1,)), ((), ())), preferred_element_type=F32)


def mm_tn(a, b):
    return lax.dot_general(a, b, (((0,), (0,)), ((), ())), preferred_element_type=F32)


def iota(shape, dim):
    return lax.broadcasted_iota(I32, shape, dim)


def norm_scale(x):
    return lax.rsqrt(jnp.mean(x * x, axis=-1, keepdims=True) + EPS)


def norm_back(x, r, dn):
    return r * dn - x * (r * r * r * jnp.mean(dn * x, axis=-1, keepdims=True))


def fold(rows):
    half = rows.shape[1] // 2
    return jnp.concatenate([rows[:, :half], rows[:, half:]], axis=0)


def unfold(rows):
    n = rows.shape[0] // 2
    return jnp.concatenate([rows[:n], rows[n:]], axis=1)


def one_hot(peer, place, count):
    left = peer * (2 * CAP) + place
    ids = jnp.concatenate([left, left + jnp.where(peer < 0, 0, CAP)], axis=0)
    return jnp.where(iota((ids.shape[0], 2 * CAP * count), 1) == ids, 1.0, 0.0).astype(BF)


def as_columns(row):
    n = row.shape[1]
    return jnp.broadcast_to(row, (n, n)).T


def kernel(
    groups, slides, near,
    emb_in, vis_in, win_in, og_in, mask_in, enc_qkv_in, enc_out_in, dec_qkv_in, dec_out_in,
    out_tiles, out_enc, out_dec,
    emb, vis, win, og, mask_token, enc_qkv, enc_out, dec_qkv, dec_out,
    sbuf, rbuf, og_halo, h_send, h_halo,
    dec_a_send, dec_b_send, dec_a, dec_b,
    enc_a_send, enc_b_send, enc_a, enc_b,
    far_send, far_recv, far_own, acc_q, acc_kv, probs, load_s,
    a2a_ss, a2a_rs, halo_ss, halo_rs, near_ss, near_rs, far_ss, far_rs,
):
    s = lax.axis_index("slide")
    g = lax.axis_index("grid")
    tiles, width = emb.shape
    vis_all = vis.shape[1]
    tokens = vis_all // groups
    far = groups // near
    rb, cw = out_enc.shape
    n = lax.rem(g, near)
    f = lax.div(g, near)
    log_g = groups.bit_length() - 1
    pending = []
    loads = []
    for i, (src, dst) in enumerate((
        (vis_in, vis), (emb_in.at[0], emb), (og_in.at[0], og), (enc_qkv_in, enc_qkv),
        (dec_out_in, dec_out), (win_in, win), (enc_out_in, enc_out), (mask_in, mask_token),
        (dec_qkv_in, dec_qkv),
    )):
        loads.append((dst, pltpu.make_async_copy(src, dst, load_s.at[i])))
    for _, copy in loads[:3]:
        copy.start()

    def wrap(index, count):
        return index - count * jnp.minimum(jnp.maximum(index - (count - 1), 0), 1)

    def loaded(*refs):
        for dst, copy in loads:
            if any(dst is ref for ref in refs):
                copy.wait()

    barrier = pltpu.get_barrier_semaphore()
    met = 0
    for j in range(1, groups):
        pl.semaphore_signal(
            barrier, inc=1, device_id=(s, wrap(g + j, groups)), device_id_type=MESH
        )
        met += 1
    for ds in range(1, slides):
        for dn in range(near):
            peer = (wrap(s + ds, slides), f * near + wrap(n + dn, near))
            pl.semaphore_signal(barrier, inc=1, device_id=peer, device_id_type=MESH)
            met += 1

    def send(src, dst, ss, rs, peer):
        copy = pltpu.make_async_remote_copy(
            src_ref=src, dst_ref=dst, send_sem=ss, recv_sem=rs,
            device_id=peer, device_id_type=MESH,
        )
        copy.start()

    def take(like, sem):
        pltpu.make_async_copy(like, like, sem).wait()

    def all_to_all_start(stage):
        for j in sorted(range(1, groups), key=lambda j: -min(j, groups - j)):
            dst = wrap(g + j, groups)
            send(sbuf.at[stage, dst], rbuf.at[stage, g], a2a_ss.at[stage], a2a_rs.at[stage],
                 (s, dst))
        rbuf[stage, g] = sbuf[stage, g]
        pending.append((sbuf.at[stage, pl.ds(0, groups - 1)], a2a_ss.at[stage]))

    def all_to_all_wait(stage):
        take(rbuf.at[stage, pl.ds(0, groups - 1)], a2a_rs.at[stage])
        return rbuf[stage].reshape(groups * 2 * CAP, width // 2)

    def halo_copies(kind, src, dst):
        left = jnp.maximum(g - 1, 0)
        right = jnp.minimum(g + 1, groups - 1)

        def to(side, peer):
            return pltpu.make_async_remote_copy(
                src_ref=src, dst_ref=dst.at[side], send_sem=halo_ss.at[kind, side],
                recv_sem=halo_rs.at[kind, side], device_id=(s, peer), device_id_type=MESH,
            )

        return to(1, left), to(0, right)

    def halo_start(kind, src, dst):
        to_left, to_right = halo_copies(kind, src, dst)

        @pl.when(g > 0)
        def _():
            to_left.start()

        @pl.when(g < groups - 1)
        def _():
            to_right.start()

    def halo_wait(kind, src, dst):
        to_left, to_right = halo_copies(kind, src, dst)

        @pl.when(g > 0)
        def _():
            to_right.wait_recv()

        @pl.when(g == 0)
        def _():
            dst[0] = jnp.zeros(dst.shape[1:], dst.dtype)

        @pl.when(g < groups - 1)
        def _():
            to_left.wait_recv()

        @pl.when(g == groups - 1)
        def _():
            dst[1] = jnp.zeros(dst.shape[1:], dst.dtype)

    def halo_end(kind, src, dst):
        to_left, to_right = halo_copies(kind, src, dst)

        @pl.when(g > 0)
        def _():
            to_left.wait_send()

        @pl.when(g < groups - 1)
        def _():
            to_right.wait_send()

    def near_start(kind, src, dst, by_slide):
        for ds in range(slides):
            for dn in range(near):
                o = ds * near + dn
                s2, n2 = wrap(s + ds, slides), wrap(n + dn, near)
                part = src.at[s2] if by_slide else src.at[n2]
                if o == 0:
                    dst[0] = part[...]
                else:
                    send(part, dst.at[o], near_ss.at[kind], near_rs.at[kind],
                         (s2, f * near + n2))
        pending.append((dst.at[pl.ds(1, slides * near - 1)], near_ss.at[kind]))

    def near_wait(kind, dst):
        take(dst.at[pl.ds(1, slides * near - 1)], near_rs.at[kind])

    def far_start(which, part):
        cube = part.reshape(far, rb, cw)
        far_own[...] = cube
        far_send[which] = cube.astype(far_send.dtype)
        for df in range(1, far):
            f2 = wrap(f + df, far)
            send(far_send.at[which, f2], far_recv.at[which, df], far_ss.at[which],
                 far_rs.at[which], (s, f2 * near + n))
        if far > 1:
            pending.append((far_send.at[which, pl.ds(1, far - 1)], far_ss.at[which]))
        return far_own[f]

    def far_end(own, which):
        if far > 1:
            take(far_recv.at[which, pl.ds(1, far - 1)], far_rs.at[which])
        total = own
        for df in range(1, far):
            total = total + far_recv[which, df].astype(F32)
        return total

    def near_product(a, b):
        return mm_tn(a[...].reshape(-1, a.shape[2]), b[...].reshape(-1, b.shape[2]))

    loaded(vis)
    vis_row = vis[...]
    t_col = g * tiles + iota((tiles, 1), 0)

    def is_visible(ids):
        return jnp.sum(jnp.where(vis_row == ids, 1.0, 0.0), axis=1, keepdims=True)

    rank = jnp.sum(jnp.where(vis_row < t_col, 1.0, 0.0), axis=1, keepdims=True).astype(I32)
    here = is_visible(t_col)
    peer = jnp.where(here > 0.5, jnp.bitwise_and(rank, groups - 1), -1)
    place = jnp.bitwise_and(jnp.right_shift(rank, log_g), CAP - 1)
    by_tile = one_hot(peer, place, groups)

    def to_slots(stage, by_row, rows):
        moved = mm_tn(by_row, fold(rows)).astype(BF)
        sbuf[stage] = moved.reshape(groups, 2 * CAP, width // 2)

    def from_slots(by_row, slots):
        return unfold(mm(by_row, slots))

    loaded(emb)
    for _, copy in loads[3:]:
        copy.start()
    to_slots(0, by_tile, emb[...])

    pl.semaphore_wait(barrier, met)
    all_to_all_start(0)
    loaded(og)
    halo_start(0, og, og_halo)

    rank_row = iota((tokens, vis_all), 1)
    mine = rank_row == iota((tokens, vis_all), 0) * groups + g
    token_tile = jnp.sum(
        jnp.where(mine, vis_row.astype(F32), 0.0), axis=1, keepdims=True
    ).astype(I32)
    source = jnp.right_shift(token_tile, tiles.bit_length() - 1)
    by_token = one_hot(source, jnp.bitwise_and(iota((tokens, 1), 0), CAP - 1), groups)
    grad_out = og[...]
    for k in range(slides):
        dec_b_send[k] = grad_out[:, k * cw : (k + 1) * cw]
    loaded(dec_out)
    dctx_mid = mm_nt(grad_out, dec_out[...]).astype(BF)
    new = iota((1, width), 1)
    span = far * rb
    low = jnp.bitwise_and(new, span - 1)
    old = (
        jnp.right_shift(low, rb.bit_length() - 1) * near
        + jnp.right_shift(new, span.bit_length() - 1)
    ) * rb + jnp.bitwise_and(low, rb - 1)
    shuffle = jnp.where(iota((width, width), 0) == old, 1.0, 0.0).astype(BF)

    def near_columns(values, dst, product=mm):
        moved = product(values, shuffle).astype(BF)
        for k in range(near):
            dst[k] = moved[:, k * span : (k + 1) * span]

    head_width = width // HEADS
    scale = 1.0 / math.sqrt(head_width)
    rows = HEADS * tokens
    heads = jnp.where(
        jnp.right_shift(iota((rows, width), 0), tokens.bit_length() - 1)
        == jnp.right_shift(iota((rows, width), 1), head_width.bit_length() - 1),
        1.0, 0.0,
    )
    heads_b = heads.astype(BF)

    loaded(enc_qkv, enc_out, win, mask_token, dec_qkv)
    slots = all_to_all_wait(0)

    tok = from_slots(by_token, slots)
    tok_r = norm_scale(tok)
    proj = mm((tok * tok_r).astype(BF), enc_qkv[...]).astype(BF)
    q, k, v = proj[:, :width], proj[:, width : 2 * width], proj[:, 2 * width :]
    def spread(values):
        return jnp.concatenate([values] * HEADS, axis=0) * heads_b

    def gather_heads(values):
        return jnp.sum((values * heads).reshape(HEADS, tokens, width), axis=0)

    qx = spread(q)
    logits = mm_nt(k, qx) * scale
    weights = jnp.exp(logits - jnp.max(logits, axis=0, keepdims=True))
    enc_p = weights / jnp.sum(weights, axis=0, keepdims=True)
    enc_pb = enc_p.astype(BF)
    enc_ctx = gather_heads(mm_tn(enc_pb, v)).astype(BF)
    encoded = (tok + mm(enc_ctx, enc_out[...])).astype(BF)
    to_slots(1, by_token, encoded)
    all_to_all_start(1)

    w_mid = win[:, pl.ds(pl.multiple_of(g * tiles, tiles), tiles)]
    w_low = win[:, pl.ds(pl.multiple_of(jnp.maximum(g - 1, 0) * tiles, tiles), tiles)]
    w_high = win[:, pl.ds(pl.multiple_of(jnp.minimum(g + 1, groups - 1) * tiles, tiles), tiles)]
    w_low = jnp.where(g > 0, w_low, -2)
    w_high = jnp.where(g < groups - 1, w_high, -2)
    first_w, last_w = w_mid[:, :1], w_mid[:, tiles - 1 :]
    w_a = jnp.where((w_mid == first_w) | (w_low == first_w), first_w, -1)
    w_b = jnp.where((w_mid == last_w) | (w_high == last_w), last_w, -1)
    mid_columns = as_columns(w_mid)
    in_a = mid_columns[:, :1] == first_w
    in_b = mid_columns[:, :1] == last_w
    vis_low = is_visible(t_col - tiles)
    vis_high = is_visible(t_col + tiles)
    blank = mask_token[...]
    near_columns(enc_ctx, enc_a_send)
    near_start(2, enc_a_send, enc_a, False)
    halo_wait(0, og, og_halo)
    dctx_edge = mm_nt(og_halo[...].reshape(2 * tiles, width), dec_out[...])
    dctx_low, dctx_high = dctx_edge[:tiles], dctx_edge[tiles:]
    dctx_a = jnp.where(in_a, dctx_mid.astype(F32), dctx_low).astype(BF)
    dctx_b = jnp.where(in_b, dctx_mid.astype(F32), dctx_high).astype(BF)
    lane = iota((1, 2 * head_width), 1)
    half0 = jnp.where(lane < head_width, 1.0, 0.0).astype(BF)
    half1 = jnp.where(lane < head_width, 0.0, 1.0).astype(BF)
    scaled0, scaled1 = half0 * BF(scale), half1 * BF(scale)
    at_a, at_b = w_mid == first_w, w_mid == last_w

    def same_window(row):
        same = jnp.where(as_columns(row) == row, 0.0, NEG)
        return jnp.concatenate([same, same], axis=1)

    def diagonal(values):
        return jnp.concatenate(
            [values[:head_width, :tiles], values[head_width:, tiles:]], axis=0
        )

    def window_blocks(*blocks):
        biases = [same_window(row) for _, _, _, row, _, _ in blocks]
        steps = [(pair, i) for pair in range(HEADS // 2) for i in range(len(blocks))]
        for pair, i in steps:
            block, qkv, dctx, _, keep_rows, keep_lanes = blocks[i]
            bias = biases[i]
            at = slice(pair * 2 * head_width, (pair + 1) * 2 * head_width)
            qs, ks, vs = qkv[0][:, at], qkv[1][:, at], qkv[2][:, at]
            do = dctx[:, at]
            qx = jnp.concatenate([qs * scaled0, qs * scaled1], axis=0)
            dox = jnp.concatenate([do * half0, do * half1], axis=0)
            scores = mm_nt(ks, qx) + bias
            e = jnp.exp(scores - jnp.max(scores, axis=0, keepdims=True))
            p = e * (1.0 / jnp.sum(e, axis=0, keepdims=True))
            pb = p.astype(BF)
            probs[block, pair] = pb
            dp = mm_nt(vs, dox)
            dsb = (p * (dp - jnp.sum(p * dp, axis=0, keepdims=True))).astype(BF)
            dq = diagonal(mm_tn(ks, dsb))
            dk = mm(dsb, qx)
            dv = mm(pb, dox)
            at_v = slice(width + at.start, width + at.stop)
            if keep_rows is not None:
                dq = jnp.where(keep_lanes, dq, acc_q[at])
                dk = jnp.where(keep_rows, dk, acc_kv[:, at])
                dv = jnp.where(keep_rows, dv, acc_kv[:, at_v])
            acc_q[at] = dq
            acc_kv[:, at] = dk
            acc_kv[:, at_v] = dv

    def window_context(values_of):
        pairs = []
        for pair in range(HEADS // 2):
            at = slice(pair * 2 * head_width, (pair + 1) * 2 * head_width)
            mid, low, high = [
                diagonal(mm_tn(values[:, at], probs[block, pair]))
                for block, values in enumerate(values_of)
            ]
            pairs.append(jnp.where(at_b, high, jnp.where(at_a, low, mid)))
        return jnp.concatenate(pairs, axis=0).astype(BF)

    def dec_project(values, shown):
        x = jnp.where(shown > 0.5, values.astype(F32), blank)
        r = norm_scale(x)
        out = mm((x * r).astype(BF), dec_qkv[...])
        return x, r, out

    def split3(values):
        values = values.astype(BF)
        return values[:, :width], values[:, width : 2 * width], values[:, 2 * width :]

    slots = all_to_all_wait(1)
    placed = from_slots(by_tile, slots).astype(BF)
    h_send[...] = placed
    halo_start(1, h_send, h_halo)
    x_mid, r_mid, qkv_mid = dec_project(placed, here)
    parts_mid = split3(qkv_mid)
    window_blocks((0, parts_mid, dctx_mid, w_mid, None, None))
    halo_wait(1, h_send, h_halo)
    near_start(0, dec_b_send, dec_b, True)
    _, _, qkv_edge = dec_project(
        h_halo[...].reshape(2 * tiles, width), jnp.concatenate([vis_low, vis_high], axis=0)
    )
    qkv_a = jnp.where(in_a, qkv_mid, qkv_edge[:tiles])
    qkv_b = jnp.where(in_b, qkv_mid, qkv_edge[tiles:])
    parts_a, parts_b = split3(qkv_a), split3(qkv_b)
    window_blocks(
        (1, parts_a, dctx_a, w_a, in_a, at_a), (2, parts_b, dctx_b, w_b, in_b, at_b)
    )

    grad_q = (acc_q[...].T * scale).astype(BF)
    dnormed = mm_nt(grad_q, dec_qkv[:, :width]) + mm_nt(
        acc_kv[...].astype(BF), dec_qkv[:, width:]
    )
    dinputs = norm_back(x_mid, r_mid, dnormed) + grad_out.astype(F32)
    to_slots(2, by_tile, dinputs.astype(BF))
    all_to_all_start(2)

    dec_ctx = window_context((parts_mid[2], parts_a[2], parts_b[2]))
    near_columns(dec_ctx, dec_a_send, mm_tn)
    near_start(1, dec_a_send, dec_a, False)
    grad_enc = from_slots(by_token, all_to_all_wait(2))
    grad_enc_b = grad_enc.astype(BF)
    for j in range(slides):
        enc_b_send[j] = grad_enc_b[:, j * cw : (j + 1) * cw]
    near_start(3, enc_b_send, enc_b, True)
    dox = spread(mm_nt(grad_enc_b, enc_out[...]).astype(BF))
    dp = mm_nt(v, dox)
    dsb = (enc_p * (dp - jnp.sum(enc_p * dp, axis=0, keepdims=True)) * scale).astype(BF)
    dq = gather_heads(mm_tn(dsb, k))
    dk = mm(dsb, qx)
    dv = mm(enc_pb, dox)
    dproj = jnp.concatenate([dq, dk, dv], axis=1).astype(BF)
    dn = mm_nt(dproj, enc_qkv[...]).astype(BF).astype(F32)
    dtok = (norm_back(tok, tok_r, dn) + grad_enc).astype(BF)
    to_slots(3, by_token, dtok)
    all_to_all_start(3)

    near_wait(0, dec_b)
    near_wait(1, dec_a)
    dec_own = far_start(0, near_product(dec_a, dec_b))
    near_wait(2, enc_a)
    near_wait(3, enc_b)
    enc_own = far_start(1, near_product(enc_a, enc_b))
    out_tiles[0] = from_slots(by_tile, all_to_all_wait(3)).astype(BF)
    out_dec[...] = far_end(dec_own, 0)
    out_enc[...] = far_end(enc_own, 1)
    for like, sem in pending:
        take(like, sem)
    halo_end(0, og, og_halo)
    halo_end(1, h_send, h_halo)


def shards(groups, slides, emb, vis, win, og, mask_token, enc_qkv, enc_out, dec_qkv, dec_out):
    _, tiles, width = emb.shape
    tokens = vis.shape[1] // groups
    near = min(4, groups)
    far = groups // near
    rb, cw = width // groups, width // slides
    span = far * rb
    ns = near * slides
    far_type = BF if rb % 16 == 0 else F32
    dma = pltpu.SemaphoreType.DMA
    operands = [
        pltpu.with_memory_space_constraint(x, pltpu.HBM)
        for x in (emb, vis, win, og, mask_token[None, :], enc_qkv, enc_out, dec_qkv, dec_out)
    ]
    vmem = pl.BlockSpec(memory_space=pltpu.VMEM)
    return pl.pallas_call(
        functools.partial(kernel, groups, slides, near),
        out_shape=(
            jax.ShapeDtypeStruct(emb.shape, BF),
            jax.ShapeDtypeStruct((rb, cw), F32),
            jax.ShapeDtypeStruct((rb, cw), F32),
        ),
        in_specs=[pl.BlockSpec(memory_space=pl.ANY)] * 9,
        out_specs=(vmem,) * 3,
        scratch_shapes=[
            pltpu.VMEM((tiles, width), BF),
            pltpu.VMEM(vis.shape, I32),
            pltpu.VMEM(win.shape, I32),
            pltpu.VMEM((tiles, width), BF),
            pltpu.VMEM((1, width), F32),
            pltpu.VMEM(enc_qkv.shape, BF),
            pltpu.VMEM(enc_out.shape, BF),
            pltpu.VMEM(dec_qkv.shape, BF),
            pltpu.VMEM(dec_out.shape, BF),
            pltpu.VMEM((4, groups, 2 * CAP, width // 2), BF),
            pltpu.VMEM((4, groups, 2 * CAP, width // 2), BF),
            pltpu.VMEM((2, tiles, width), BF),
            pltpu.VMEM((tiles, width), BF),
            pltpu.VMEM((2, tiles, width), BF),
            pltpu.VMEM((near, tiles, span), BF),
            pltpu.VMEM((slides, tiles, cw), BF),
            pltpu.VMEM((ns, tiles, span), BF),
            pltpu.VMEM((ns, tiles, cw), BF),
            pltpu.VMEM((near, tokens, span), BF),
            pltpu.VMEM((slides, tokens, cw), BF),
            pltpu.VMEM((ns, tokens, span), BF),
            pltpu.VMEM((ns, tokens, cw), BF),
            pltpu.VMEM((2, far, rb, cw), far_type),
            pltpu.VMEM((2, far, rb, cw), far_type),
            pltpu.VMEM((far, rb, cw), F32),
            pltpu.VMEM((width, tiles), F32),
            pltpu.VMEM((tiles, 2 * width), F32),
            pltpu.VMEM((3, HEADS // 2, tiles, 2 * tiles), BF),
            dma((9,)),
            dma((4,)), dma((4,)),
            dma((2, 2)), dma((2, 2)),
            dma((4,)), dma((4,)),
            dma((2,)), dma((2,)),
        ],
        compiler_params=pltpu.CompilerParams(
            collective_id=0, has_side_effects=True, vmem_limit_bytes=44 * 1024 * 1024
        ),
    )(*operands)


def solution(mesh):
    placed = (
        P("slide", "grid", None),
        P("slide", None),
        P("slide", None),
        P("slide", "grid", None),
        P(),
        P(),
        P(),
        P(),
        P(),
    )
    return jax.shard_map(
        functools.partial(shards, mesh.shape["grid"], mesh.shape["slide"]),
        mesh=mesh,
        in_specs=placed,
        out_specs=(P("slide", "grid", None), P("grid", "slide"), P("grid", "slide")),
        check_vma=False,
    )
```

```python
import functools
import math

import jax
import jax.numpy as jnp
from jax import lax
from jax.experimental import pallas as pl
from jax.experimental.pallas import tpu as pltpu
from jax.sharding import PartitionSpec as P

HEADS = 8
EPS = 1e-06
CAP = 8
NEG = -1e30
BF = jnp.bfloat16
F32 = jnp.float32
I32 = jnp.int32
MESH = pl.DeviceIdType.MESH


def mm(a, b):
    return lax.dot_general(a, b, (((1,), (0,)), ((), ())), preferred_element_type=F32)


def mm_nt(a, b):
    return lax.dot_general(a, b, (((1,), (1,)), ((), ())), preferred_element_type=F32)


def mm_tn(a, b):
    return lax.dot_general(a, b, (((0,), (0,)), ((), ())), preferred_element_type=F32)


def iota(shape, dim):
    return lax.broadcasted_iota(I32, shape, dim)


def norm_scale(x):
    return lax.rsqrt(jnp.mean(x * x, axis=-1, keepdims=True) + EPS)


def norm_back(x, r, dn):
    return r * dn - x * (r * r * r * jnp.mean(dn * x, axis=-1, keepdims=True))


def fold(rows):
    half = rows.shape[1] // 2
    return jnp.concatenate([rows[:, :half], rows[:, half:]], axis=0)


def unfold(rows):
    n = rows.shape[0] // 2
    return jnp.concatenate([rows[:n], rows[n:]], axis=1)


def one_hot(peer, place, count):
    left = peer * (2 * CAP) + place
    ids = jnp.concatenate([left, left + jnp.where(peer < 0, 0, CAP)], axis=0)
    return jnp.where(iota((ids.shape[0], 2 * CAP * count), 1) == ids, 1.0, 0.0).astype(BF)


def as_columns(row):
    n = row.shape[1]
    return jnp.broadcast_to(row, (n, n)).T


def kernel(
    groups, slides, near,
    emb_in, vis_in, win_in, og_in, mask_in, enc_qkv_in, enc_out_in, dec_qkv_in, dec_out_in,
    out_tiles, out_enc, out_dec,
    emb, vis, win, og, mask_token, enc_qkv, enc_out, dec_qkv, dec_out,
    sbuf, rbuf, og_halo, h_send, h_halo,
    dec_a_send, dec_b_send, dec_a, dec_b,
    enc_a_send, enc_b_send, enc_a, enc_b,
    far_send, far_recv, far_own, acc_q, acc_kv, probs, load_s,
    a2a_ss, a2a_rs, halo_ss, halo_rs, near_ss, near_rs, far_ss, far_rs,
):
    s = lax.axis_index("slide")
    g = lax.axis_index("grid")
    tiles, width = emb.shape
    vis_all = vis.shape[1]
    tokens = vis_all // groups
    far = groups // near
    rb, cw = out_enc.shape
    n = lax.rem(g, near)
    f = lax.div(g, near)
    log_g = groups.bit_length() - 1
    pending = []
    loads = []
    for i, (src, dst) in enumerate((
        (vis_in, vis), (emb_in.at[0], emb), (og_in.at[0], og), (enc_qkv_in, enc_qkv),
        (dec_out_in, dec_out), (win_in, win), (enc_out_in, enc_out), (mask_in, mask_token),
        (dec_qkv_in, dec_qkv),
    )):
        loads.append((dst, pltpu.make_async_copy(src, dst, load_s.at[i])))
    for _, copy in loads[:3]:
        copy.start()

    def wrap(index, count):
        return index - count * jnp.minimum(jnp.maximum(index - (count - 1), 0), 1)

    def loaded(*refs):
        for dst, copy in loads:
            if any(dst is ref for ref in refs):
                copy.wait()

    barrier = pltpu.get_barrier_semaphore()
    met = 0
    for j in range(1, groups):
        pl.semaphore_signal(
            barrier, inc=1, device_id=(s, wrap(g + j, groups)), device_id_type=MESH
        )
        met += 1
    for ds in range(1, slides):
        for dn in range(near):
            peer = (wrap(s + ds, slides), f * near + wrap(n + dn, near))
            pl.semaphore_signal(barrier, inc=1, device_id=peer, device_id_type=MESH)
            met += 1

    def send(src, dst, ss, rs, peer):
        copy = pltpu.make_async_remote_copy(
            src_ref=src, dst_ref=dst, send_sem=ss, recv_sem=rs,
            device_id=peer, device_id_type=MESH,
        )
        copy.start()

    def take(like, sem):
        pltpu.make_async_copy(like, like, sem).wait()

    def all_to_all_start(stage):
        for j in sorted(range(1, groups), key=lambda j: -min(j, groups - j)):
            dst = wrap(g + j, groups)
            send(sbuf.at[stage, dst], rbuf.at[stage, g], a2a_ss.at[stage], a2a_rs.at[stage],
                 (s, dst))
        rbuf[stage, g] = sbuf[stage, g]
        pending.append((sbuf.at[stage, pl.ds(0, groups - 1)], a2a_ss.at[stage]))

    def all_to_all_wait(stage):
        take(rbuf.at[stage, pl.ds(0, groups - 1)], a2a_rs.at[stage])
        return rbuf[stage].reshape(groups * 2 * CAP, width // 2)

    def halo_copies(kind, src, dst):
        left = jnp.maximum(g - 1, 0)
        right = jnp.minimum(g + 1, groups - 1)

        def to(side, peer):
            return pltpu.make_async_remote_copy(
                src_ref=src, dst_ref=dst.at[side], send_sem=halo_ss.at[kind, side],
                recv_sem=halo_rs.at[kind, side], device_id=(s, peer), device_id_type=MESH,
            )

        return to(1, left), to(0, right)

    def halo_start(kind, src, dst):
        to_left, to_right = halo_copies(kind, src, dst)

        @pl.when(g > 0)
        def _():
            to_left.start()

        @pl.when(g < groups - 1)
        def _():
            to_right.start()

    def halo_wait(kind, src, dst):
        to_left, to_right = halo_copies(kind, src, dst)

        @pl.when(g > 0)
        def _():
            to_right.wait_recv()

        @pl.when(g == 0)
        def _():
            dst[0] = jnp.zeros(dst.shape[1:], dst.dtype)

        @pl.when(g < groups - 1)
        def _():
            to_left.wait_recv()

        @pl.when(g == groups - 1)
        def _():
            dst[1] = jnp.zeros(dst.shape[1:], dst.dtype)

    def halo_end(kind, src, dst):
        to_left, to_right = halo_copies(kind, src, dst)

        @pl.when(g > 0)
        def _():
            to_left.wait_send()

        @pl.when(g < groups - 1)
        def _():
            to_right.wait_send()

    def near_start(kind, src, dst, by_slide):
        for ds in range(slides):
            for dn in range(near):
                o = ds * near + dn
                s2, n2 = wrap(s + ds, slides), wrap(n + dn, near)
                part = src.at[s2] if by_slide else src.at[n2]
                if o == 0:
                    dst[0] = part[...]
                else:
                    send(part, dst.at[o], near_ss.at[kind], near_rs.at[kind],
                         (s2, f * near + n2))
        pending.append((dst.at[pl.ds(1, slides * near - 1)], near_ss.at[kind]))

    def near_wait(kind, dst):
        take(dst.at[pl.ds(1, slides * near - 1)], near_rs.at[kind])

    def far_start(which, part):
        cube = part.reshape(far, rb, cw)
        far_own[...] = cube
        far_send[which] = cube.astype(far_send.dtype)
        for df in range(1, far):
            f2 = wrap(f + df, far)
            send(far_send.at[which, f2], far_recv.at[which, df], far_ss.at[which],
                 far_rs.at[which], (s, f2 * near + n))
        if far > 1:
            pending.append((far_send.at[which, pl.ds(1, far - 1)], far_ss.at[which]))
        return far_own[f]

    def far_end(own, which):
        if far > 1:
            take(far_recv.at[which, pl.ds(1, far - 1)], far_rs.at[which])
        total = own
        for df in range(1, far):
            total = total + far_recv[which, df].astype(F32)
        return total

    def near_product(a, b):
        return mm_tn(a[...].reshape(-1, a.shape[2]), b[...].reshape(-1, b.shape[2]))

    loaded(vis)
    vis_row = vis[...]
    t_col = g * tiles + iota((tiles, 1), 0)

    def is_visible(ids):
        return jnp.sum(jnp.where(vis_row == ids, 1.0, 0.0), axis=1, keepdims=True)

    rank = jnp.sum(jnp.where(vis_row < t_col, 1.0, 0.0), axis=1, keepdims=True).astype(I32)
    here = is_visible(t_col)
    peer = jnp.where(here > 0.5, jnp.bitwise_and(rank, groups - 1), -1)
    place = jnp.bitwise_and(jnp.right_shift(rank, log_g), CAP - 1)
    by_tile = one_hot(peer, place, groups)

    def to_slots(stage, by_row, rows):
        moved = mm_tn(by_row, fold(rows)).astype(BF)
        sbuf[stage] = moved.reshape(groups, 2 * CAP, width // 2)

    def from_slots(by_row, slots):
        return unfold(mm(by_row, slots))

    loaded(emb)
    for _, copy in loads[3:]:
        copy.start()
    to_slots(0, by_tile, emb[...])

    pl.semaphore_wait(barrier, met)
    all_to_all_start(0)
    loaded(og)
    halo_start(0, og, og_halo)

    rank_row = iota((tokens, vis_all), 1)
    mine = rank_row == iota((tokens, vis_all), 0) * groups + g
    token_tile = jnp.sum(
        jnp.where(mine, vis_row.astype(F32), 0.0), axis=1, keepdims=True
    ).astype(I32)
    source = jnp.right_shift(token_tile, tiles.bit_length() - 1)
    by_token = one_hot(source, jnp.bitwise_and(iota((tokens, 1), 0), CAP - 1), groups)
    grad_out = og[...]
    for k in range(slides):
        dec_b_send[k] = grad_out[:, k * cw : (k + 1) * cw]
    loaded(dec_out)
    dctx_mid = mm_nt(grad_out, dec_out[...]).astype(BF)
    new = iota((1, width), 1)
    span = far * rb
    low = jnp.bitwise_and(new, span - 1)
    old = (
        jnp.right_shift(low, rb.bit_length() - 1) * near
        + jnp.right_shift(new, span.bit_length() - 1)
    ) * rb + jnp.bitwise_and(low, rb - 1)
    shuffle = jnp.where(iota((width, width), 0) == old, 1.0, 0.0).astype(BF)

    def near_columns(values, dst, product=mm):
        moved = product(values, shuffle).astype(BF)
        for k in range(near):
            dst[k] = moved[:, k * span : (k + 1) * span]

    head_width = width // HEADS
    scale = 1.0 / math.sqrt(head_width)
    rows = HEADS * tokens
    heads = jnp.where(
        jnp.right_shift(iota((rows, width), 0), tokens.bit_length() - 1)
        == jnp.right_shift(iota((rows, width), 1), head_width.bit_length() - 1),
        1.0, 0.0,
    )
    heads_b = heads.astype(BF)

    loaded(enc_qkv, enc_out, win, mask_token, dec_qkv)
    slots = all_to_all_wait(0)

    tok = from_slots(by_token, slots)
    tok_r = norm_scale(tok)
    proj = mm((tok * tok_r).astype(BF), enc_qkv[...]).astype(BF)
    q, k, v = proj[:, :width], proj[:, width : 2 * width], proj[:, 2 * width :]
    def spread(values):
        return jnp.concatenate([values] * HEADS, axis=0) * heads_b

    def gather_heads(values):
        return jnp.sum((values * heads).reshape(HEADS, tokens, width), axis=0)

    qx = spread(q)
    logits = mm_nt(k, qx) * scale
    weights = jnp.exp(logits - jnp.max(logits, axis=0, keepdims=True))
    enc_p = weights / jnp.sum(weights, axis=0, keepdims=True)
    enc_pb = enc_p.astype(BF)
    enc_ctx = gather_heads(mm_tn(enc_pb, v)).astype(BF)
    encoded = (tok + mm(enc_ctx, enc_out[...])).astype(BF)
    to_slots(1, by_token, encoded)
    all_to_all_start(1)

    w_mid = win[:, pl.ds(pl.multiple_of(g * tiles, tiles), tiles)]
    w_low = win[:, pl.ds(pl.multiple_of(jnp.maximum(g - 1, 0) * tiles, tiles), tiles)]
    w_high = win[:, pl.ds(pl.multiple_of(jnp.minimum(g + 1, groups - 1) * tiles, tiles), tiles)]
    w_low = jnp.where(g > 0, w_low, -2)
    w_high = jnp.where(g < groups - 1, w_high, -2)
    first_w, last_w = w_mid[:, :1], w_mid[:, tiles - 1 :]
    w_a = jnp.where((w_mid == first_w) | (w_low == first_w), first_w, -1)
    w_b = jnp.where((w_mid == last_w) | (w_high == last_w), last_w, -1)
    mid_columns = as_columns(w_mid)
    in_a = mid_columns[:, :1] == first_w
    in_b = mid_columns[:, :1] == last_w
    vis_low = is_visible(t_col - tiles)
    vis_high = is_visible(t_col + tiles)
    blank = mask_token[...]
    near_columns(enc_ctx, enc_a_send)
    near_start(2, enc_a_send, enc_a, False)
    halo_wait(0, og, og_halo)
    dctx_edge = mm_nt(og_halo[...].reshape(2 * tiles, width), dec_out[...])
    dctx_low, dctx_high = dctx_edge[:tiles], dctx_edge[tiles:]
    dctx_a = jnp.where(in_a, dctx_mid.astype(F32), dctx_low).astype(BF)
    dctx_b = jnp.where(in_b, dctx_mid.astype(F32), dctx_high).astype(BF)
    lane = iota((1, 2 * head_width), 1)
    half0 = jnp.where(lane < head_width, 1.0, 0.0).astype(BF)
    half1 = jnp.where(lane < head_width, 0.0, 1.0).astype(BF)
    scaled0, scaled1 = half0 * BF(scale), half1 * BF(scale)
    at_a, at_b = w_mid == first_w, w_mid == last_w

    def same_window(row):
        same = jnp.where(as_columns(row) == row, 0.0, NEG)
        return jnp.concatenate([same, same], axis=1)

    def diagonal(values):
        return jnp.concatenate(
            [values[:head_width, :tiles], values[head_width:, tiles:]], axis=0
        )

    def window_blocks(*blocks):
        biases = [same_window(row) for _, _, _, row, _, _ in blocks]
        steps = [(pair, i) for pair in range(HEADS // 2) for i in range(len(blocks))]
        for pair, i in steps:
            block, qkv, dctx, _, keep_rows, keep_lanes = blocks[i]
            bias = biases[i]
            at = slice(pair * 2 * head_width, (pair + 1) * 2 * head_width)
            qs, ks, vs = qkv[0][:, at], qkv[1][:, at], qkv[2][:, at]
            do = dctx[:, at]
            qx = jnp.concatenate([qs * scaled0, qs * scaled1], axis=0)
            dox = jnp.concatenate([do * half0, do * half1], axis=0)
            scores = mm_nt(ks, qx) + bias
            e = jnp.exp(scores - jnp.max(scores, axis=0, keepdims=True))
            p = e * (1.0 / jnp.sum(e, axis=0, keepdims=True))
            pb = p.astype(BF)
            probs[block, pair] = pb
            dp = mm_nt(vs, dox)
            dsb = (p * (dp - jnp.sum(p * dp, axis=0, keepdims=True))).astype(BF)
            dq = diagonal(mm_tn(ks, dsb))
            dk = mm(dsb, qx)
            dv = mm(pb, dox)
            at_v = slice(width + at.start, width + at.stop)
            if keep_rows is not None:
                dq = jnp.where(keep_lanes, dq, acc_q[at])
                dk = jnp.where(keep_rows, dk, acc_kv[:, at])
                dv = jnp.where(keep_rows, dv, acc_kv[:, at_v])
            acc_q[at] = dq
            acc_kv[:, at] = dk
            acc_kv[:, at_v] = dv

    def window_context(values_of):
        pairs = []
        for pair in range(HEADS // 2):
            at = slice(pair * 2 * head_width, (pair + 1) * 2 * head_width)
            mid, low, high = [
                diagonal(mm_tn(values[:, at], probs[block, pair]))
                for block, values in enumerate(values_of)
            ]
            pairs.append(jnp.where(at_b, high, jnp.where(at_a, low, mid)))
        return jnp.concatenate(pairs, axis=0).astype(BF)

    def dec_project(values, shown):
        x = jnp.where(shown > 0.5, values.astype(F32), blank)
        r = norm_scale(x)
        out = mm((x * r).astype(BF), dec_qkv[...])
        return x, r, out

    def split3(values):
        values = values.astype(BF)
        return values[:, :width], values[:, width : 2 * width], values[:, 2 * width :]

    slots = all_to_all_wait(1)
    placed = from_slots(by_tile, slots).astype(BF)
    h_send[...] = placed
    halo_start(1, h_send, h_halo)
    x_mid, r_mid, qkv_mid = dec_project(placed, here)
    parts_mid = split3(qkv_mid)
    window_blocks((0, parts_mid, dctx_mid, w_mid, None, None))
    halo_wait(1, h_send, h_halo)
    near_start(0, dec_b_send, dec_b, True)
    _, _, qkv_edge = dec_project(
        h_halo[...].reshape(2 * tiles, width), jnp.concatenate([vis_low, vis_high], axis=0)
    )
    qkv_a = jnp.where(in_a, qkv_mid, qkv_edge[:tiles])
    qkv_b = jnp.where(in_b, qkv_mid, qkv_edge[tiles:])
    parts_a, parts_b = split3(qkv_a), split3(qkv_b)
    window_blocks(
        (1, parts_a, dctx_a, w_a, in_a, at_a), (2, parts_b, dctx_b, w_b, in_b, at_b)
    )

    grad_q = (acc_q[...].T * scale).astype(BF)
    dnormed = mm_nt(grad_q, dec_qkv[:, :width]) + mm_nt(
        acc_kv[...].astype(BF), dec_qkv[:, width:]
    )
    dinputs = norm_back(x_mid, r_mid, dnormed) + grad_out.astype(F32)
    to_slots(2, by_tile, dinputs.astype(BF))
    all_to_all_start(2)

    dec_ctx = window_context((parts_mid[2], parts_a[2], parts_b[2]))
    near_columns(dec_ctx, dec_a_send, mm_tn)
    grad_enc = from_slots(by_token, all_to_all_wait(2))
    grad_enc_b = grad_enc.astype(BF)
    for j in range(slides):
        enc_b_send[j] = grad_enc_b[:, j * cw : (j + 1) * cw]
    near_start(3, enc_b_send, enc_b, True)
    near_start(1, dec_a_send, dec_a, False)
    dox = spread(mm_nt(grad_enc_b, enc_out[...]).astype(BF))
    dp = mm_nt(v, dox)
    dsb = (enc_p * (dp - jnp.sum(enc_p * dp, axis=0, keepdims=True)) * scale).astype(BF)
    dq = gather_heads(mm_tn(dsb, k))
    dk = mm(dsb, qx)
    dv = mm(enc_pb, dox)
    dproj = jnp.concatenate([dq, dk, dv], axis=1).astype(BF)
    dn = mm_nt(dproj, enc_qkv[...]).astype(BF).astype(F32)
    dtok = (norm_back(tok, tok_r, dn) + grad_enc).astype(BF)
    to_slots(3, by_token, dtok)
    all_to_all_start(3)

    near_wait(0, dec_b)
    near_wait(1, dec_a)
    dec_own = far_start(0, near_product(dec_a, dec_b))
    near_wait(2, enc_a)
    near_wait(3, enc_b)
    enc_own = far_start(1, near_product(enc_a, enc_b))
    out_tiles[0] = from_slots(by_tile, all_to_all_wait(3)).astype(BF)
    out_dec[...] = far_end(dec_own, 0)
    out_enc[...] = far_end(enc_own, 1)
    for like, sem in pending:
        take(like, sem)
    halo_end(0, og, og_halo)
    halo_end(1, h_send, h_halo)


def shards(groups, slides, emb, vis, win, og, mask_token, enc_qkv, enc_out, dec_qkv, dec_out):
    _, tiles, width = emb.shape
    tokens = vis.shape[1] // groups
    near = min(4, groups)
    far = groups // near
    rb, cw = width // groups, width // slides
    span = far * rb
    ns = near * slides
    far_type = BF if rb % 16 == 0 else F32
    dma = pltpu.SemaphoreType.DMA
    operands = [
        pltpu.with_memory_space_constraint(x, pltpu.HBM)
        for x in (emb, vis, win, og, mask_token[None, :], enc_qkv, enc_out, dec_qkv, dec_out)
    ]
    vmem = pl.BlockSpec(memory_space=pltpu.VMEM)
    return pl.pallas_call(
        functools.partial(kernel, groups, slides, near),
        out_shape=(
            jax.ShapeDtypeStruct(emb.shape, BF),
            jax.ShapeDtypeStruct((rb, cw), F32),
            jax.ShapeDtypeStruct((rb, cw), F32),
        ),
        in_specs=[pl.BlockSpec(memory_space=pl.ANY)] * 9,
        out_specs=(vmem,) * 3,
        scratch_shapes=[
            pltpu.VMEM((tiles, width), BF),
            pltpu.VMEM(vis.shape, I32),
            pltpu.VMEM(win.shape, I32),
            pltpu.VMEM((tiles, width), BF),
            pltpu.VMEM((1, width), F32),
            pltpu.VMEM(enc_qkv.shape, BF),
            pltpu.VMEM(enc_out.shape, BF),
            pltpu.VMEM(dec_qkv.shape, BF),
            pltpu.VMEM(dec_out.shape, BF),
            pltpu.VMEM((4, groups, 2 * CAP, width // 2), BF),
            pltpu.VMEM((4, groups, 2 * CAP, width // 2), BF),
            pltpu.VMEM((2, tiles, width), BF),
            pltpu.VMEM((tiles, width), BF),
            pltpu.VMEM((2, tiles, width), BF),
            pltpu.VMEM((near, tiles, span), BF),
            pltpu.VMEM((slides, tiles, cw), BF),
            pltpu.VMEM((ns, tiles, span), BF),
            pltpu.VMEM((ns, tiles, cw), BF),
            pltpu.VMEM((near, tokens, span), BF),
            pltpu.VMEM((slides, tokens, cw), BF),
            pltpu.VMEM((ns, tokens, span), BF),
            pltpu.VMEM((ns, tokens, cw), BF),
            pltpu.VMEM((2, far, rb, cw), far_type),
            pltpu.VMEM((2, far, rb, cw), far_type),
            pltpu.VMEM((far, rb, cw), F32),
            pltpu.VMEM((width, tiles), F32),
            pltpu.VMEM((tiles, 2 * width), F32),
            pltpu.VMEM((3, HEADS // 2, tiles, 2 * tiles), BF),
            dma((9,)),
            dma((4,)), dma((4,)),
            dma((2, 2)), dma((2, 2)),
            dma((4,)), dma((4,)),
            dma((2,)), dma((2,)),
        ],
        compiler_params=pltpu.CompilerParams(
            collective_id=0, has_side_effects=True, vmem_limit_bytes=44 * 1024 * 1024
        ),
    )(*operands)


def solution(mesh):
    placed = (
        P("slide", "grid", None),
        P("slide", None),
        P("slide", None),
        P("slide", "grid", None),
        P(),
        P(),
        P(),
        P(),
        P(),
    )
    return jax.shard_map(
        functools.partial(shards, mesh.shape["grid"], mesh.shape["slide"]),
        mesh=mesh,
        in_specs=placed,
        out_specs=(P("slide", "grid", None), P("grid", "slide"), P("grid", "slide")),
        check_vma=False,
    )
```
